256 devices in a mesh: role: 2 (over z_hi), dp: 8 (over x, core), fsdp: 16 (over y, z_lo).
Axes of the slice: x: 4, y: 4, z: 8 (z_hi: 2, z_lo: 4; z = z_hi * 4 + z_lo), core: 2. Of those that a mesh axis runs over, the one named last changes fastest.
Arguments:
- rows: bfloat16 [128, 256, 2048], P(('dp', 'fsdp'), 'role'), may hold values from -40 to 40
- cotangent: bfloat16 [128, 256, 2048], P(('dp', 'fsdp'), 'role'), may hold values from -6 to 6
- advantage: float32 [128, 256], P(('dp', 'fsdp'), 'role'), may hold values from -4 to 4
- action: int32 [128, 256], P(('dp', 'fsdp'), 'role'), may hold values 0 or 1
- norm_gain: float32 [2048], replicated, may hold values from 0.5 to 1.5
- q_gain: float32 [128], replicated, may hold values from 0.6 to 5.2
- k_gain: float32 [128], replicated, may hold values from 0.6 to 5.2
- w_q: bfloat16 [2048, 2048], P('fsdp', 'role'), may hold values from -0.1016466 to 0.1016466
- w_k: bfloat16 [2048, 512], P('fsdp', 'role'), may hold values from -0.1016466 to 0.1016466
- w_v: bfloat16 [2048, 512], P('fsdp', 'role'), may hold values from -0.125 to 0.125
- w_o: bfloat16 [2048, 2048], P('role', 'fsdp'), may hold values from -0.125 to 0.125
Outputs:
- out_rows: bfloat16 [128, 256, 2048], P(('dp', 'fsdp'), 'role')
- grad_rows: bfloat16 [128, 256, 2048], P(('dp', 'fsdp'), 'role')
- grad_w_q: float32 [2048, 2048], P('fsdp', 'role')
- grad_w_k: float32 [2048, 512], P('fsdp', 'role')
- grad_w_v: float32 [2048, 512], P('fsdp', 'role')
- grad_w_o: float32 [2048, 2048], P('role', 'fsdp')
The draws below stay inside these ranges and needn't reach their ends.
All inputs are finite; a program needn't handle non-finite values. No bound on the sum of `action` on one device may be relied on, other than what follows from the above.
Results may differ from the reference program's by a relative error of at most 0.04.
The reference program's roundings to bfloat16 on the way count: a program that leaves them out, or rounds other values in their place, can miss the bound.
Values may be sent and summed in bfloat16 or wider, within the bound.
No kernel may reach another device: no remote copies, remote signals or barrier semaphores. Data moves between devices by JAX's collectives and lax.ppermute only.
A program may use at most 128 MiB of HBM per device.

```python
from functools import partial
import jax
import jax.numpy as jnp
from jax import lax

D = 2048
HEADS = 16
KV = 4
HD = 128
TRAJ = 128
PAIRS = 128
PAIR_ROWS = 256
N_ROLE = 2


def draw_rows(key, part):
    own_key = jax.random.fold_in(key, 13)
    key_base, key_row, key_col = jax.random.split(own_key, 3)
    full_shape = (PAIRS, PAIR_ROWS, D)
    base = jax.random.truncated_normal(key_base, -4.0, 4.0, full_shape, jnp.float32)
    row_scale = jnp.exp(jax.random.uniform(key_row, (PAIRS, PAIR_ROWS, 1), jnp.float32, jnp.log(0.3), jnp.log(3.0)))
    col_scale = jnp.exp(jax.random.uniform(key_col, (1, 1, D), jnp.float32, jnp.log(0.3), jnp.log(3.0)))
    return jnp.clip(base * row_scale * col_scale, -40.0, 40.0).astype(jnp.bfloat16)


def gain_draw(key, salt):
    own_key = jax.random.fold_in(key, salt)
    return jax.random.uniform(own_key, (HD,), jnp.float32, 0.6, 1.6)


def draw_q_gain(key, part):
    return gain_draw(key, 21)


def draw_k_gain(key, part):
    return gain_draw(key, 22)


def weight_pair(key):
    own_key = jax.random.fold_in(key, 31)
    key_keys, key_query = jax.random.split(own_key, 2)
    base_keys = jax.random.truncated_normal(key_keys, -4.5, 4.5, (D, KV * HD), jnp.float32)
    base_query = jax.random.truncated_normal(key_query, -4.5, 4.5, (D, HEADS * HD), jnp.float32)
    return (base_keys, base_query)


def draw_w_k(key, part):
    base_keys, base_query = weight_pair(key)
    return (base_keys * D ** (-0.5)).astype(jnp.bfloat16)


def draw_w_q(key, part):
    base_keys, base_query = weight_pair(key)
    return (base_query * D ** (-0.5)).astype(jnp.bfloat16)


def plant(drawn, key, smallest, largest):
    extent = drawn.shape
    spot = [jax.random.randint(jax.random.fold_in(key, axis), (), 0, extent[axis]) for axis in range(len(extent))]
    drawn = drawn.at[tuple(spot)].set(smallest)
    longest = extent.index(max(extent))
    spot[longest] = (spot[longest] + 1) % extent[longest]
    return drawn.at[tuple(spot)].set(largest)


def block_levels(key, shape, shards, least, top_value):
    gain, own = 1.0, jax.random.fold_in(key, 6)
    for dim, shards_of in shards:
        draws = jnp.exp(jax.random.uniform(jax.random.fold_in(own, dim), (shards_of,), jnp.float32, least / len(shards), top_value / len(shards)))
        gain = gain * jnp.repeat(draws, shape[dim] // shards_of).reshape([-1 if axis == dim else 1 for axis in range(len(shape))])
    return gain


def scatter_about(key, extent, spread, bound, pieces=(), kind=jnp.bfloat16):
    result = jax.random.normal(key, extent, jnp.float32) * spread
    if len(pieces) > 0:
        result = block_levels(key, extent, pieces, -0.22, 0.18) * result
    return jnp.clip(result, min=-bound, max=bound).astype(kind)


def setup_inputs(seed: int = 0) -> dict:
    key_of = jax.random.split(jax.random.key(seed), 12)
    rows = draw_rows(jax.random.fold_in(key_of[11], 71), 0)
    cotangent = scatter_about(key_of[1], (PAIRS, PAIR_ROWS, D), 1.0, 6.0, ((0, 128), (1, 2)))
    advantage = scatter_about(key_of[2], (PAIRS, PAIR_ROWS), 1.0, 4.0, ((0, 128), (1, 2)), jnp.float32)
    action = plant((jax.random.randint(key_of[3], (PAIRS, PAIR_ROWS), 0, 3) < 1).astype(jnp.int32), jax.random.fold_in(key_of[3], 1), 0, 1)
    norm_gain = jnp.clip(1.0 + 0.1 * jax.random.normal(key_of[4], (D,), jnp.float32), 0.5, 1.5)
    q_gain = draw_q_gain(jax.random.fold_in(key_of[11], 71), 0)
    k_gain = draw_k_gain(jax.random.fold_in(key_of[11], 71), 0)
    w_q = draw_w_q(jax.random.fold_in(key_of[11], 71), 0)
    w_k = draw_w_k(jax.random.fold_in(key_of[11], 71), 0)
    w_v = scatter_about(key_of[9], (D, KV * HD), D ** -0.5, 0.125, ((0, 16), (1, 2)))
    w_o = scatter_about(key_of[10], (HEADS * HD, D), (HEADS * HD) ** -0.5, 0.125, ((0, 2), (1, 16)))
    return dict(rows=rows, cotangent=cotangent, advantage=advantage, action=action, norm_gain=norm_gain, q_gain=q_gain, k_gain=k_gain, w_q=w_q, w_k=w_k, w_v=w_v, w_o=w_o)


eps_norm = 1e-06
theta_base = 1000000.0

def rope_tables(row_count, traj_len, head_width):
    middle = head_width // 2
    position = (jnp.arange(row_count, dtype=jnp.int32) % traj_len).astype(jnp.float32)
    inverse = jnp.exp(jnp.arange(middle, dtype=jnp.float32) * (-2.0 * jnp.log(jnp.float32(theta_base)) / head_width))
    angles = position[:, None] * inverse[None, :]
    return (jnp.cos(angles), jnp.sin(angles))

def head_shape(values, gain_vec, cosine, sine_tab):
    middle = values.shape[-1] // 2
    mean_square = lax.optimization_barrier(jnp.mean(values * values, axis=-1, keepdims=True))
    normal_vals = values * lax.rsqrt(mean_square + eps_norm) * gain_vec
    former = normal_vals[..., :middle]
    latter = normal_vals[..., middle:]
    cos_mid = cosine[:, None, :]
    sin_mid = sine_tab[:, None, :]
    return jnp.concatenate([former * cos_mid - latter * sin_mid, latter * cos_mid + former * sin_mid], axis=-1)

def causal_mask(traj_len):
    return jnp.arange(traj_len)[:, None] >= jnp.arange(traj_len)[None, :]

def attend(query_rot, key_rot, value_b, traj_len):
    rows_all, heads_here, head_width = query_rot.shape
    kv_here = key_rot.shape[1]
    seq_count = rows_all // traj_len
    query_five = query_rot.reshape(seq_count, traj_len, kv_here, heads_here // kv_here, head_width)
    key_four = key_rot.reshape(seq_count, traj_len, kv_here, head_width)
    value_four = value_b.reshape(seq_count, traj_len, kv_here, head_width)
    scores = jnp.einsum('tiaqd,tjad->taqij', query_five.astype(jnp.float32), key_four.astype(jnp.float32)) * head_width ** (-0.5)
    allowed = causal_mask(traj_len)
    scores = jnp.where(allowed, scores, -1e+30)
    peak = lax.optimization_barrier(jnp.max(scores, axis=-1, keepdims=True))
    weights = jnp.where(allowed, jnp.exp(scores - peak), 0.0)
    probs = weights / lax.optimization_barrier(jnp.sum(weights, axis=-1, keepdims=True))
    probs_b = probs.astype(jnp.bfloat16)
    mixed = jnp.einsum('taqij,tjad->tiaqd', probs_b.astype(jnp.float32), value_four.astype(jnp.float32)).astype(jnp.bfloat16)
    return (probs, probs_b, mixed.reshape(rows_all, heads_here * head_width))

def attend_back(grad_mixed, probs, probs_b, query_rot, key_rot, value_b, traj_len):
    rows_all, heads_here, head_width = query_rot.shape
    kv_here = key_rot.shape[1]
    seq_count = rows_all // traj_len
    group_size = heads_here // kv_here
    query_five = query_rot.reshape(seq_count, traj_len, kv_here, group_size, head_width).astype(jnp.float32)
    key_four = key_rot.reshape(seq_count, traj_len, kv_here, head_width).astype(jnp.float32)
    value_four = value_b.reshape(seq_count, traj_len, kv_here, head_width).astype(jnp.float32)
    grad_five = grad_mixed.reshape(seq_count, traj_len, kv_here, group_size, head_width).astype(jnp.float32)
    grad_probs = jnp.einsum('tiaqd,tjad->taqij', grad_five, value_four)
    grad_value = jnp.einsum('taqij,tiaqd->tjad', probs_b.astype(jnp.float32), grad_five).astype(jnp.bfloat16)
    grad_scores = (probs * (grad_probs - lax.optimization_barrier(jnp.sum(grad_probs * probs, axis=-1, keepdims=True))) * head_width ** (-0.5)).astype(jnp.bfloat16)
    grad_query = jnp.einsum('taqij,tjad->tiaqd', grad_scores.astype(jnp.float32), key_four)
    grad_key = jnp.einsum('taqij,tiaqd->tjad', grad_scores.astype(jnp.float32), query_five)
    return (grad_query.reshape(rows_all, heads_here, head_width), grad_key.reshape(rows_all, kv_here, head_width), grad_value.reshape(rows_all, kv_here * head_width))

def rounded(values):
    return lax.optimization_barrier(values.astype(jnp.bfloat16)).astype(jnp.float32)

def reference(rows, cotangent, advantage, action, norm_gain, q_gain, k_gain, w_q, w_k, w_v, w_o):
    pair_rows = rows.shape[1]
    cos_tab, sin_tab = rope_tables(pair_rows, TRAJ, HD)
    gain_full = norm_gain.astype(jnp.float32)
    per_role = HEADS * HD // N_ROLE
    kv_role = KV * HD // N_ROLE

    def one_pair(totals, batch):
        x_pair, cot_pair, adv_pair, act_pair = batch
        x_full = x_pair.astype(jnp.float32)
        inv_rms = lax.rsqrt(lax.optimization_barrier(jnp.mean(x_full * x_full, axis=-1, keepdims=True)) + eps_norm)
        normed = (x_full * inv_rms * gain_full).astype(jnp.bfloat16)
        query = jnp.dot(normed, w_q, preferred_element_type=jnp.float32).reshape(pair_rows, HEADS, HD)
        keys = jnp.dot(normed, w_k, preferred_element_type=jnp.float32).reshape(pair_rows, KV, HD)
        value_b = jnp.dot(normed, w_v, preferred_element_type=jnp.float32).astype(jnp.bfloat16).reshape(pair_rows, KV, HD)
        q_rot, pull_query = jax.vjp(partial(head_shape, gain_vec=q_gain, cosine=cos_tab, sine_tab=sin_tab), query)
        k_rot, pull_keys = jax.vjp(partial(head_shape, gain_vec=k_gain, cosine=cos_tab, sine_tab=sin_tab), keys)
        query_rot = q_rot.astype(jnp.bfloat16)
        key_rot = k_rot.astype(jnp.bfloat16)
        probs, probs_b, mixed = attend(query_rot, key_rot, value_b, TRAJ)
        blocks = jnp.einsum('rnc,ncd->nrd', mixed.reshape(pair_rows, N_ROLE, per_role).astype(jnp.float32), w_o.reshape(N_ROLE, per_role, D).astype(jnp.float32))
        out_rows = (x_full + lax.optimization_barrier(jnp.sum(rounded(blocks), axis=0))).astype(jnp.bfloat16)
        grad_out = (cot_pair.astype(jnp.float32) * (adv_pair * act_pair.astype(jnp.float32))[:, None]).astype(jnp.bfloat16)
        grad_mixed = jnp.dot(grad_out, w_o.T, preferred_element_type=jnp.float32).astype(jnp.bfloat16)
        grad_q_rot, grad_k_rot, grad_value = attend_back(grad_mixed, probs, probs_b, query_rot, key_rot, value_b, TRAJ)
        grad_query = pull_query(grad_q_rot)[0].astype(jnp.bfloat16).reshape(pair_rows, HEADS * HD)
        grad_keys = pull_keys(grad_k_rot)[0].astype(jnp.bfloat16).reshape(pair_rows, KV * HD)
        shares = jnp.einsum('rnc,dnc->nrd', grad_query.reshape(pair_rows, N_ROLE, per_role).astype(jnp.float32), w_q.reshape(D, N_ROLE, per_role).astype(jnp.float32))
        shares = shares + jnp.einsum('rnc,dnc->nrd', grad_keys.reshape(pair_rows, N_ROLE, kv_role).astype(jnp.float32), w_k.reshape(D, N_ROLE, kv_role).astype(jnp.float32))
        shares = shares + jnp.einsum('rnc,dnc->nrd', grad_value.reshape(pair_rows, N_ROLE, kv_role).astype(jnp.float32), w_v.reshape(D, N_ROLE, kv_role).astype(jnp.float32))
        grad_normed = lax.optimization_barrier(jnp.sum(rounded(shares), axis=0))
        scaled = grad_normed * gain_full
        unit_rows = x_full * inv_rms
        grad_rows = (grad_out.astype(jnp.float32) + inv_rms * (scaled - unit_rows * lax.optimization_barrier(jnp.mean(scaled * unit_rows, axis=-1, keepdims=True)))).astype(jnp.bfloat16)
        term_q = jnp.dot(normed.T, grad_query, preferred_element_type=jnp.float32)
        term_k = jnp.dot(normed.T, grad_keys, preferred_element_type=jnp.float32)
        term_v = jnp.dot(normed.T, grad_value, preferred_element_type=jnp.float32)
        term_o = jnp.dot(mixed.T, grad_out, preferred_element_type=jnp.float32)
        new_totals = (totals[0] + rounded(term_q), totals[1] + rounded(term_k), totals[2] + rounded(term_v), totals[3] + rounded(term_o))
        return (new_totals, (out_rows, grad_rows))
    start_totals = (jnp.zeros((D, HEADS * HD), jnp.float32), jnp.zeros((D, KV * HD), jnp.float32), jnp.zeros((D, KV * HD), jnp.float32), jnp.zeros((HEADS * HD, D), jnp.float32))
    totals, stacked = lax.scan(one_pair, start_totals, (rows, cotangent, advantage, action))
    return (stacked[0], stacked[1], totals[0], totals[1], totals[2], totals[3])
```

```python
from functools import partial

import jax
import jax.numpy as jnp
from jax import lax
from jax.sharding import PartitionSpec as P

HD = 128
TRAJ = 128
NX = 4
NC = 2
NY = 4
NZ = 4

eps_norm = 1e-06
theta_base = 1000000.0
f32 = jnp.float32
bf16 = jnp.bfloat16


def rope_tables(row_count, traj_len, head_width):
    middle = head_width // 2
    position = (jnp.arange(row_count, dtype=jnp.int32) % traj_len).astype(jnp.float32)
    inverse = jnp.exp(
        jnp.arange(middle, dtype=jnp.float32)
        * (-2.0 * jnp.log(jnp.float32(theta_base)) / head_width)
    )
    angles = position[:, None] * inverse[None, :]
    return (jnp.cos(angles), jnp.sin(angles))


def head_shape(values, gain_vec, cosine, sine_tab):
    middle = values.shape[-1] // 2
    mean_square = jnp.mean(values * values, axis=-1, keepdims=True)
    normal_vals = values * lax.rsqrt(mean_square + eps_norm) * gain_vec
    former = normal_vals[..., :middle]
    latter = normal_vals[..., middle:]
    cos_mid = cosine[:, None, :]
    sin_mid = sine_tab[:, None, :]
    return jnp.concatenate(
        [former * cos_mid - latter * sin_mid, latter * cos_mid + former * sin_mid], axis=-1
    )


def causal_mask(traj_len):
    return jnp.arange(traj_len)[:, None] >= jnp.arange(traj_len)[None, :]


def attend(query_rot, key_rot, value_b, traj_len):
    rows_all, heads_here, head_width = query_rot.shape
    kv_here = key_rot.shape[1]
    seq_count = rows_all // traj_len
    query_five = query_rot.reshape(seq_count, traj_len, kv_here, heads_here // kv_here, head_width)
    key_four = key_rot.reshape(seq_count, traj_len, kv_here, head_width)
    value_four = value_b.reshape(seq_count, traj_len, kv_here, head_width)
    scores = jnp.einsum(
        "tiaqd,tjad->taqij", query_five, key_four, preferred_element_type=jnp.float32
    ) * head_width ** (-0.5)
    allowed = causal_mask(traj_len)
    scores = jnp.where(allowed, scores, -1e30)
    peak = jnp.max(scores, axis=-1, keepdims=True)
    weights = jnp.where(allowed, jnp.exp(scores - peak), 0.0)
    probs = weights / jnp.sum(weights, axis=-1, keepdims=True)
    probs_b = probs.astype(jnp.bfloat16)
    mixed = jnp.einsum(
        "taqij,tjad->tiaqd", probs_b, value_four, preferred_element_type=jnp.float32
    ).astype(jnp.bfloat16)
    return (probs, probs_b, mixed.reshape(rows_all, heads_here * head_width))


def attend_back(grad_mixed, probs, probs_b, query_rot, key_rot, value_b, traj_len):
    rows_all, heads_here, head_width = query_rot.shape
    kv_here = key_rot.shape[1]
    seq_count = rows_all // traj_len
    group_size = heads_here // kv_here
    query_five = query_rot.reshape(seq_count, traj_len, kv_here, group_size, head_width)
    key_four = key_rot.reshape(seq_count, traj_len, kv_here, head_width)
    value_four = value_b.reshape(seq_count, traj_len, kv_here, head_width)
    grad_five = grad_mixed.reshape(seq_count, traj_len, kv_here, group_size, head_width)
    grad_probs = jnp.einsum(
        "tiaqd,tjad->taqij", grad_five, value_four, preferred_element_type=jnp.float32
    )
    grad_value = jnp.einsum(
        "taqij,tiaqd->tjad", probs_b, grad_five, preferred_element_type=jnp.float32
    ).astype(jnp.bfloat16)
    grad_scores = (
        probs
        * (grad_probs - jnp.sum(grad_probs * probs, axis=-1, keepdims=True))
        * head_width ** (-0.5)
    ).astype(jnp.bfloat16)
    grad_query = jnp.einsum(
        "taqij,tjad->tiaqd", grad_scores, key_four, preferred_element_type=jnp.float32
    )
    grad_key = jnp.einsum(
        "taqij,tiaqd->tjad", grad_scores, query_five, preferred_element_type=jnp.float32
    )
    return (
        grad_query.reshape(rows_all, heads_here, head_width),
        grad_key.reshape(rows_all, kv_here, head_width),
        grad_value.reshape(rows_all, kv_here * head_width),
    )


def dot_rows(left, right):
    return lax.dot_general(left, right, (((1,), (1,)), ((), ())), preferred_element_type=f32)


def dot_cols(left, right):
    return lax.dot_general(left, right, (((0,), (0,)), ((), ())), preferred_element_type=f32)


def dot(left, right):
    return jnp.dot(left, right, preferred_element_type=f32)


def take_x(value, step):
    pairs = [
        (x * NC + c, (x - step) % NX * NC + c) for x in range(NX) for c in range(NC)
    ]
    return lax.ppermute(value, "dp", pairs)


def take_y(value, step):
    pairs = [(y * NZ + z, (y - step) % NY * NZ + z) for y in range(NY) for z in range(NZ)]
    return lax.ppermute(value, "fsdp", pairs)


def take_z(value, step):
    pairs = [(y * NZ + z, y * NZ + (z - step) % NZ) for y in range(NY) for z in range(NZ)]
    return lax.ppermute(value, "fsdp", pairs)


def other_core(value):
    return lax.ppermute(value, "dp", [(i, i ^ 1) for i in range(NX * NC)])


def owner_role(x):
    return x // (NX // 2)


def from_owner(value):
    n = NX * NC
    pairs = [(owner_role(d // NC) * n + d, (1 - owner_role(d // NC)) * n + d) for d in range(n)]
    return lax.ppermute(value, ("role", "dp"), pairs)


def to_owner(value):
    n = NX * NC
    pairs = [((1 - owner_role(d // NC)) * n + d, owner_role(d // NC) * n + d) for d in range(n)]
    return lax.ppermute(value, ("role", "dp"), pairs)


def spread_x(value, step):
    n = NX * NC
    pairs = [
        (owner_role(x) * n + x * NC + c, owner_role(x) * n + (x - step) % NX * NC + c)
        for x in range(NX)
        for c in range(NC)
    ]
    return lax.ppermute(value, ("role", "dp"), pairs)


def turn(value, y, z):
    rows = value.shape[0]
    blocks = value.reshape(rows, NY, NZ, HD)
    twice = jnp.concatenate([blocks, blocks], axis=1)
    blocks = lax.dynamic_slice_in_dim(twice, y, NY, axis=1)
    twice = jnp.concatenate([blocks, blocks], axis=2)
    blocks = lax.dynamic_slice_in_dim(twice, z, NZ, axis=2)
    return blocks.reshape(rows, NY * NZ * HD)


def gather_weight(block, at_owner):
    block = jnp.where(at_owner, block, from_owner(block))
    plane = jnp.concatenate([block] + [take_z(block, k) for k in range(1, NZ)], axis=0)
    own = [plane] + [take_y(plane, k) for k in range(1, NY)]
    other = [other_core(piece) for piece in own]
    return own, other


def sum_weight(own, other_cols, at_owner, x, role):
    term = (own.astype(f32) + other_core(other_cols).astype(f32)).astype(bf16)
    span = term.shape[0] // NY
    total = term[:span].astype(f32)
    for k in range(1, NY):
        total = total + take_y(term[k * span : (k + 1) * span], -k).astype(f32)
    term = total.astype(bf16)
    span = span // NZ
    total = term[:span].astype(f32)
    for k in range(1, NZ):
        total = total + take_z(term[k * span : (k + 1) * span], -k).astype(f32)
    term = total.astype(bf16)
    total = (term.astype(f32) + to_owner(term).astype(f32)).astype(bf16)
    copies = [total] + [spread_x(total, k) for k in range(1, NX)]
    items = []
    for sub in range(2):
        source = role * 2 + sub
        item = copies[0]
        for k in range(1, NX):
            item = jnp.where((source - x) % NX == k, copies[k], item)
        items.append(item)
    mine = jnp.concatenate(items, axis=0)
    return mine, other_core(mine)


def on_device(rows, cotangent, advantage, action, norm_gain, q_gain, k_gain, w_q, w_k, w_v, w_o):
    role = lax.axis_index("role")
    dp = lax.axis_index("dp")
    fsdp = lax.axis_index("fsdp")
    x, core = dp // NC, dp % NC
    y, z = fsdp // NZ, fsdp % NZ
    at_owner = role == owner_role(x)
    sub = x % 2
    width = 4 * HD
    half = 2 * HD
    first = core == 0

    q_part = lax.dynamic_slice(w_q, (0, sub * width + core * half), (HD, half))
    k_part = lax.dynamic_slice(w_k, (0, sub * HD), (HD, HD))
    v_part = lax.dynamic_slice(w_v, (0, sub * HD), (HD, HD))
    qkv_block = jnp.concatenate([q_part, jnp.where(first, k_part, v_part)], axis=1)
    o_block = lax.dynamic_slice(w_o, (sub * width + core * half, 0), (half, HD)).T
    qkv_own, qkv_other = gather_weight(qkv_block, at_owner)
    o_own, o_other = gather_weight(o_block, at_owner)

    x_own = rows[0].astype(f32)
    inv_own = lax.rsqrt(jnp.mean(x_own * x_own, axis=-1, keepdims=True) + eps_norm)
    normed_own = turn((x_own * inv_own * norm_gain).astype(bf16), y, z)
    grad_own = (
        cotangent[0].astype(f32) * (advantage[0] * action[0].astype(f32))[:, None]
    ).astype(bf16)
    grad_turned = turn(grad_own, y, z)
    normed = jnp.concatenate([normed_own] + [take_x(normed_own, k) for k in range(1, NX)], axis=0)
    grad_all = jnp.concatenate([grad_turned] + [take_x(grad_turned, k) for k in range(1, NX)], axis=0)

    w_own, w_other = jnp.concatenate(qkv_own, axis=0), jnp.concatenate(qkv_other, axis=0)
    wo_own, wo_other = jnp.concatenate(o_own, axis=0), jnp.concatenate(o_other, axis=0)
    proj_own, proj_other = dot(normed, w_own), dot(normed, w_other)
    tokens = normed.shape[0]
    query = jnp.concatenate([proj_own[:, :half], proj_other[:, :half]], axis=1).reshape(tokens, 4, HD)
    tail_own, tail_other = proj_own[:, half:], proj_other[:, half:]
    keys = jnp.where(first, tail_own, tail_other).reshape(tokens, 1, HD)
    value_b = jnp.where(first, tail_other, tail_own).astype(bf16).reshape(tokens, 1, HD)
    cos_tab, sin_tab = rope_tables(tokens, TRAJ, HD)
    q_rot, pull_query = jax.vjp(
        partial(head_shape, gain_vec=q_gain, cosine=cos_tab, sine_tab=sin_tab), query
    )
    k_rot, pull_keys = jax.vjp(
        partial(head_shape, gain_vec=k_gain, cosine=cos_tab, sine_tab=sin_tab), keys
    )
    query_rot = q_rot.astype(bf16)
    key_rot = k_rot.astype(bf16)
    probs, probs_b, mixed = attend(query_rot, key_rot, value_b, TRAJ)

    part_out = (dot_rows(mixed[:, :half], wo_own) + dot_rows(mixed[:, half:], wo_other)).astype(bf16)
    head_total = part_out[:TRAJ].astype(f32)
    for k in range(1, NX):
        head_total = head_total + take_x(part_out[k * TRAJ : (k + 1) * TRAJ], -k).astype(f32)
    head_total = turn(head_total, (NY - y) % NY, (NZ - z) % NZ)
    out_rows = (x_own + head_total).astype(bf16)

    grad_mixed = jnp.concatenate([dot(grad_all, wo_own), dot(grad_all, wo_other)], axis=1).astype(bf16)
    grad_q_rot, grad_k_rot, grad_value = attend_back(
        grad_mixed, probs, probs_b, query_rot, key_rot, value_b, TRAJ
    )
    grad_query = pull_query(grad_q_rot)[0].astype(bf16).reshape(tokens, width)
    grad_keys = pull_keys(grad_k_rot)[0].astype(bf16).reshape(tokens, HD)
    g_own = jnp.concatenate([grad_query[:, :half], jnp.where(first, grad_keys, grad_value)], axis=1)
    g_other = jnp.concatenate([grad_query[:, half:], jnp.where(first, grad_value, grad_keys)], axis=1)
    back = (dot_rows(g_own, w_own) + dot_rows(g_other, w_other)).astype(bf16)
    grad_normed = back[:TRAJ].astype(f32)
    for k in range(1, NX):
        grad_normed = grad_normed + take_x(back[k * TRAJ : (k + 1) * TRAJ], -k).astype(f32)
    grad_normed = turn(grad_normed, (NY - y) % NY, (NZ - z) % NZ)
    scaled = grad_normed * norm_gain
    unit_rows = x_own * inv_own
    grad_rows = (
        grad_own.astype(f32)
        + inv_own * (scaled - unit_rows * jnp.mean(scaled * unit_rows, axis=-1, keepdims=True))
    ).astype(bf16)

    go_mine, go_theirs = sum_weight(
        dot_cols(grad_all, mixed[:, :half]).astype(bf16),
        dot_cols(grad_all, mixed[:, half:]).astype(bf16),
        at_owner,
        x,
        role,
    )
    gw_mine, gw_theirs = sum_weight(
        dot_cols(normed, g_own).astype(bf16), dot_cols(normed, g_other).astype(bf16), at_owner, x, role
    )
    gw_0, gw_1 = jnp.where(first, gw_mine, gw_theirs), jnp.where(first, gw_theirs, gw_mine)
    go_0, go_1 = jnp.where(first, go_mine, go_theirs), jnp.where(first, go_theirs, go_mine)

    def pick(value, item, lo, hi):
        return value[item * HD : (item + 1) * HD, lo:hi].astype(f32)

    grad_w_q = jnp.concatenate(
        [pick(gw, item, 0, half) for item in range(2) for gw in (gw_0, gw_1)], axis=1
    )
    grad_w_k = jnp.concatenate([pick(gw_0, item, half, half + HD) for item in range(2)], axis=1)
    grad_w_v = jnp.concatenate([pick(gw_1, item, half, half + HD) for item in range(2)], axis=1)
    grad_w_o = jnp.concatenate(
        [pick(go, item, 0, half).T for item in range(2) for go in (go_0, go_1)], axis=0
    )
    return (out_rows[None], grad_rows[None], grad_w_q, grad_w_k, grad_w_v, grad_w_o)


def solution(mesh):
    in_specs = (
        P(("dp", "fsdp"), "role", None),
        P(("dp", "fsdp"), "role", None),
        P(("dp", "fsdp"), "role"),
        P(("dp", "fsdp"), "role"),
        P(),
        P(),
        P(),
        P("fsdp", "role"),
        P("fsdp", "role"),
        P("fsdp", "role"),
        P("role", "fsdp"),
    )
    out_specs = (
        P(("dp", "fsdp"), "role", None),
        P(("dp", "fsdp"), "role", None),
        P("fsdp", "role"),
        P("fsdp", "role"),
        P("fsdp", "role"),
        P("role", "fsdp"),
    )
    return jax.shard_map(
        on_device, mesh=mesh, in_specs=in_specs, out_specs=out_specs, check_vma=False
    )
```

```python
import jax
import jax.numpy as jnp
from jax import lax
from jax.experimental import pallas as pl
from jax.experimental.pallas import tpu as pltpu
from jax.sharding import PartitionSpec as P

HD = 128
TRAJ = 128
NX = 4
NC = 2
NY = 4
NZ = 4

eps_norm = 1e-06
theta_base = 1000000.0
f32 = jnp.float32
bf16 = jnp.bfloat16


def dims(a, b, left, right):
    return lax.dot_general(left, right, (((a,), (b,)), ((), ())), preferred_element_type=f32)


def dot(left, right):
    return dims(1, 0, left, right)


def dot_rows(left, right):
    return dims(1, 1, left, right)


def dot_cols(left, right):
    return dims(0, 0, left, right)


def call(kernel, outs, vmem, scalars=1, **more):
    return pl.pallas_call(
        kernel,
        out_shape=[jax.ShapeDtypeStruct(shape, kind) for shape, kind in outs],
        in_specs=[pl.BlockSpec(memory_space=pltpu.SMEM)] * scalars
        + [pl.BlockSpec(memory_space=pltpu.VMEM)] * (vmem - scalars),
        out_specs=[pl.BlockSpec(memory_space=pltpu.VMEM)] * len(outs),
        compiler_params=pltpu.CompilerParams(vmem_limit_bytes=40 << 20),
        **more,
    )


def turned(place_ref, j):
    row = lax.rem(place_ref[0] + j // NZ, NY)
    col = lax.rem(place_ref[1] + j % NZ, NZ)
    return pl.ds(pl.multiple_of((row * NZ + col) * HD, HD), HD)


def norm_kernel(place_ref, rows_ref, gain_ref, normed_ref):
    x = rows_ref[...].astype(f32)
    inv = lax.rsqrt(jnp.mean(x * x, axis=-1, keepdims=True) + eps_norm)
    for j in range(NY * NZ):
        at = turned(place_ref, j)
        normed_ref[:, j * HD : (j + 1) * HD] = (
            rows_ref[:, at].astype(f32) * inv * gain_ref[:, at]
        ).astype(bf16)


def weigh_kernel(place_ref, cot_ref, weight_ref, grad_ref):
    weight = weight_ref[...]
    for j in range(NY * NZ):
        at = turned(place_ref, j)
        grad_ref[:, j * HD : (j + 1) * HD] = (cot_ref[:, at].astype(f32) * weight).astype(bf16)


def total_block(parts, j):
    cols = slice(j * HD, (j + 1) * HD)
    total = parts[0][:, cols].astype(f32)
    for part in parts[1:]:
        total = total + part[:, cols].astype(f32)
    return total


def out_kernel(place_ref, rows_ref, *refs):
    parts, out_ref = refs[:NX], refs[NX]
    for j in range(NY * NZ):
        at = turned(place_ref, j)
        out_ref[:, at] = (rows_ref[:, at].astype(f32) + total_block(parts, j)).astype(bf16)


def grad_rows_kernel(place_ref, rows_ref, gain_ref, cot_ref, weight_ref, *refs):
    parts, out_ref, scaled_ref = refs[:NX], refs[NX], refs[NX + 1]
    x = rows_ref[...].astype(f32)
    inv = lax.rsqrt(jnp.mean(x * x, axis=-1, keepdims=True) + eps_norm)
    weight = weight_ref[...]
    for j in range(NY * NZ):
        at = turned(place_ref, j)
        scaled_ref[:, at] = total_block(parts, j) * gain_ref[:, at]
    scaled = scaled_ref[...]
    unit = x * inv
    mean = jnp.mean(scaled * unit, axis=-1, keepdims=True)
    grad_out = (cot_ref[...].astype(f32) * weight).astype(bf16).astype(f32)
    out_ref[...] = (grad_out + inv * (scaled - unit * mean)).astype(bf16)


def project_kernel(normed_ref, *refs):
    own, other, outs = refs[:NY], refs[NY : 2 * NY], refs[2 * NY :]
    for chunks, out_ref in zip((own, other), outs):
        total = None
        for j in range(NY):
            span = chunks[j].shape[0]
            term = dot(normed_ref[:, j * span : (j + 1) * span], chunks[j][...])
            total = term if total is None else total + term
        out_ref[...] = total.astype(out_ref.dtype)


def expand_kernel(left_own_ref, left_other_ref, *refs):
    own, other, outs = refs[:NY], refs[NY : 2 * NY], refs[2 * NY :]
    for j in range(NY):
        span = own[j].shape[0]
        total = dot_rows(left_own_ref[...], own[j][...]) + dot_rows(left_other_ref[...], other[j][...])
        for k in range(NX):
            outs[k][:, j * span : (j + 1) * span] = total[k * TRAJ : (k + 1) * TRAJ].astype(bf16)


def rotate(t, cos, sin):
    return t * cos + pltpu.roll(t, HD // 2, 1) * sin


def rotate_back(g, cos, sin):
    return g * cos + pltpu.roll(g * sin, HD // 2, 1)


def inv_norm(t):
    return lax.rsqrt(jnp.mean(t * t, axis=-1, keepdims=True) + eps_norm)


def norm_back(t, grad, gain):
    r = inv_norm(t)
    u = grad * gain
    return r * u - t * (r * r * r * jnp.mean(t * u, axis=-1, keepdims=True))


def stack_heads(own_ref, other_ref):
    return jnp.concatenate(
        [ref[:, k * HD : (k + 1) * HD] for ref in (own_ref, other_ref) for k in range(2)], axis=0
    )


def attend_kernel(
    first_ref, own_ref, other_ref, q_gain_ref, k_gain_ref, cos_ref, sin_ref,
    q_rot_ref, k_rot_ref, value_ref, probs_ref, mixed_own_ref, mixed_other_ref,
):
    cos, sin = cos_ref[...], sin_ref[...]
    cos4, sin4 = jnp.concatenate([cos] * 4, axis=0), jnp.concatenate([sin] * 4, axis=0)
    first = first_ref[0] == 1
    tail_own, tail_other = own_ref[:, 2 * HD :], other_ref[:, 2 * HD :]
    keys = jnp.where(first, tail_own, tail_other)
    value = jnp.where(first, tail_other, tail_own).astype(bf16)
    query = stack_heads(own_ref, other_ref)
    q_rot = rotate(query * inv_norm(query) * q_gain_ref[...], cos4, sin4).astype(bf16)
    k_rot = rotate(keys * inv_norm(keys) * k_gain_ref[...], cos, sin).astype(bf16)
    scores = dot_rows(q_rot, k_rot) * HD ** (-0.5)
    row = lax.broadcasted_iota(jnp.int32, scores.shape, 0) % TRAJ
    allowed = row >= lax.broadcasted_iota(jnp.int32, scores.shape, 1)
    scores = jnp.where(allowed, scores, -1e30)
    peak = jnp.max(scores, axis=-1, keepdims=True)
    weights = jnp.where(allowed, jnp.exp(scores - peak), 0.0)
    probs = weights / jnp.sum(weights, axis=-1, keepdims=True)
    mixed = dot(probs.astype(bf16), value).astype(bf16)
    q_rot_ref[...] = q_rot
    k_rot_ref[...] = k_rot
    value_ref[...] = value
    probs_ref[...] = probs
    for k in range(2):
        mixed_own_ref[:, k * HD : (k + 1) * HD] = mixed[k * TRAJ : (k + 1) * TRAJ]
        mixed_other_ref[:, k * HD : (k + 1) * HD] = mixed[(k + 2) * TRAJ : (k + 3) * TRAJ]


def attend_back_kernel(
    first_ref, own_ref, other_ref, q_gain_ref, k_gain_ref, cos_ref, sin_ref,
    q_rot_ref, k_rot_ref, value_ref, probs_ref, gm_own_ref, gm_other_ref,
    g_own_ref, g_other_ref,
):
    cos, sin = cos_ref[...], sin_ref[...]
    cos4, sin4 = jnp.concatenate([cos] * 4, axis=0), jnp.concatenate([sin] * 4, axis=0)
    first = first_ref[0] == 1
    keys = jnp.where(first, own_ref[:, 2 * HD :], other_ref[:, 2 * HD :])
    query = stack_heads(own_ref, other_ref)
    grad_mixed = stack_heads(gm_own_ref, gm_other_ref)
    q_rot, k_rot, value, probs = q_rot_ref[...], k_rot_ref[...], value_ref[...], probs_ref[...]
    grad_probs = dot_rows(grad_mixed, value)
    grad_value = dot_cols(probs.astype(bf16), grad_mixed).astype(bf16)
    inner = jnp.sum(grad_probs * probs, axis=-1, keepdims=True)
    grad_scores = (probs * (grad_probs - inner) * HD ** (-0.5)).astype(bf16)
    grad_q_rot = dot(grad_scores, k_rot)
    grad_k_rot = dot_cols(grad_scores, q_rot)
    grad_query = norm_back(query, rotate_back(grad_q_rot, cos4, sin4), q_gain_ref[...]).astype(bf16)
    grad_keys = norm_back(keys, rotate_back(grad_k_rot, cos, sin), k_gain_ref[...]).astype(bf16)
    for k in range(2):
        g_own_ref[:, k * HD : (k + 1) * HD] = grad_query[k * TRAJ : (k + 1) * TRAJ]
        g_other_ref[:, k * HD : (k + 1) * HD] = grad_query[(k + 2) * TRAJ : (k + 3) * TRAJ]
    g_own_ref[:, 2 * HD :] = jnp.where(first, grad_keys, grad_value)
    g_other_ref[:, 2 * HD :] = jnp.where(first, grad_value, grad_keys)


def by_trajectory(kernel, outs, ins):
    def spec(rows, cols):
        if rows == 0:
            return pl.BlockSpec(cols, lambda i: (0, 0))
        return pl.BlockSpec((rows, cols), lambda i: (i, 0))

    return pl.pallas_call(
        kernel,
        grid=(NX,),
        out_shape=[jax.ShapeDtypeStruct((rows * NX, cols), kind) for rows, cols, kind in outs],
        in_specs=[pl.BlockSpec(memory_space=pltpu.SMEM)] + [spec(*entry) for entry in ins],
        out_specs=[spec(rows, cols) for rows, cols, _ in outs],
        compiler_params=pltpu.CompilerParams(vmem_limit_bytes=40 << 20),
    )


def weight_grad_kernel(left_ref, own_ref, other_ref, *refs):
    outs, other_out = refs[:NY], refs[NY]
    for j in range(NY):
        span = outs[j].shape[0]
        left = left_ref[:, j * span : (j + 1) * span]
        other_out[j * span : (j + 1) * span] = dot_cols(left, other_ref[...]).astype(bf16)
        outs[j][...] = dot_cols(left, own_ref[...]).astype(bf16)


def rope_tables():
    position = jnp.arange(TRAJ, dtype=jnp.int32).astype(f32)
    inverse = jnp.exp(
        jnp.arange(HD // 2, dtype=f32) * (-2.0 * jnp.log(jnp.float32(theta_base)) / HD)
    )
    angles = position[:, None] * inverse[None, :]
    cos, sin = jnp.cos(angles), jnp.sin(angles)
    return jnp.concatenate([cos, cos], axis=1), jnp.concatenate([-sin, sin], axis=1)


def after(value, *earlier):
    return lax.optimization_barrier((value,) + earlier)[0]


def take_x(value, step):
    pairs = [
        (x * NC + c, (x - step) % NX * NC + c) for x in range(NX) for c in range(NC)
    ]
    return lax.ppermute(value, "dp", pairs)


def take_y(value, step):
    pairs = [(y * NZ + z, (y - step) % NY * NZ + z) for y in range(NY) for z in range(NZ)]
    return lax.ppermute(value, "fsdp", pairs)


def take_z(value, step):
    pairs = [(y * NZ + z, y * NZ + (z - step) % NZ) for y in range(NY) for z in range(NZ)]
    return lax.ppermute(value, "fsdp", pairs)


def other_core(value):
    return lax.ppermute(value, "dp", [(i, i ^ 1) for i in range(NX * NC)])


def owner_role(x):
    return x // (NX // 2)


def from_owner(value):
    n = NX * NC
    pairs = [(owner_role(d // NC) * n + d, (1 - owner_role(d // NC)) * n + d) for d in range(n)]
    return lax.ppermute(value, ("role", "dp"), pairs)


def to_owner(value):
    n = NX * NC
    pairs = [((1 - owner_role(d // NC)) * n + d, owner_role(d // NC) * n + d) for d in range(n)]
    return lax.ppermute(value, ("role", "dp"), pairs)


def spread_x(value, step):
    n = NX * NC
    pairs = [
        (owner_role(x) * n + x * NC + c, owner_role(x) * n + (x - step) % NX * NC + c)
        for x in range(NX)
        for c in range(NC)
    ]
    return lax.ppermute(value, ("role", "dp"), pairs)


def role_and_z(block, at_owner):
    block = jnp.where(at_owner, block, from_owner(block))
    return jnp.concatenate([block] + [take_z(block, k) for k in range(1, NZ)], axis=0)


def over_y(plane):
    own = [plane] + [take_y(plane, k) for k in range(1, NY)]
    return own, [other_core(piece) for piece in own]


def sum_weight(own, other_cols, at_owner, x, role):
    theirs = other_core(other_cols)
    span = own[0].shape[0]
    terms = [
        (own[k].astype(f32) + theirs[k * span : (k + 1) * span].astype(f32)) for k in range(NY)
    ]
    total = terms[0]
    for k in range(1, NY):
        total = total + take_y(terms[k].astype(bf16), -k).astype(f32)
    span = span // NZ
    term = total[:span]
    for k in range(1, NZ):
        term = term + take_z(total[k * span : (k + 1) * span].astype(bf16), -k).astype(f32)
    term = term.astype(bf16)
    total = (term.astype(f32) + to_owner(term).astype(f32)).astype(bf16)
    copies = [total] + [spread_x(total, k) for k in range(1, NX)]
    items = []
    for sub in range(2):
        source = role * 2 + sub
        item = copies[0]
        for k in range(1, NX):
            item = jnp.where((source - x) % NX == k, copies[k], item)
        items.append(item)
    mine = jnp.concatenate(items, axis=0)
    return mine, other_core(mine)


def on_device(rows, cotangent, advantage, action, norm_gain, q_gain, k_gain, w_q, w_k, w_v, w_o):
    role = lax.axis_index("role")
    dp = lax.axis_index("dp")
    fsdp = lax.axis_index("fsdp")
    x, core = dp // NC, dp % NC
    y, z = fsdp // NZ, fsdp % NZ
    at_owner = role == owner_role(x)
    sub = x % 2
    width = 4 * HD
    half = 2 * HD
    first = core == 0
    place = jnp.stack([y, z]).astype(jnp.int32)
    flag = first.astype(jnp.int32)[None]

    q_part = lax.dynamic_slice(w_q, (0, sub * width + core * half), (HD, half))
    k_part = lax.dynamic_slice(w_k, (0, sub * HD), (HD, HD))
    v_part = lax.dynamic_slice(w_v, (0, sub * HD), (HD, HD))
    qkv_block = jnp.concatenate([q_part, jnp.where(first, k_part, v_part)], axis=1)
    qkv_plane = role_and_z(qkv_block, at_owner)
    qkv_own, qkv_other = over_y(qkv_plane)

    o_block = lax.dynamic_slice(w_o, (sub * width + core * half, 0), (half, HD)).T
    o_plane = role_and_z(after(o_block, qkv_plane), at_owner)
    o_own, o_other = over_y(after(o_plane, *qkv_own))

    rows_own, cot_own = rows[0], cotangent[0]
    gain = norm_gain[None]
    weight = (advantage[0] * action[0].astype(f32))[:, None]
    flat = (TRAJ, rows_own.shape[1])
    normed_own = call(norm_kernel, [(flat, bf16)], 3)(place, rows_own, gain)[0]
    normed_parts = [normed_own] + [take_x(normed_own, k) for k in range(1, NX)]
    normed = jnp.concatenate(normed_parts, axis=0)
    grad_turned = call(weigh_kernel, [(flat, bf16)], 3)(place, cot_own, weight)[0]
    grad_turned = after(grad_turned, *normed_parts)
    grad_all = jnp.concatenate(
        [grad_turned] + [take_x(grad_turned, k) for k in range(1, NX)], axis=0
    )

    tokens = normed.shape[0]
    wide = half + HD
    cos_tab, sin_tab = rope_tables()
    proj_own, proj_other = call(
        project_kernel, [((tokens, wide), f32)] * 2, 1 + 2 * NY, scalars=0
    )(normed, *qkv_own, *qkv_other)
    shared = [(0, (1, HD)), (0, (1, HD)), (0, (TRAJ, HD)), (0, (TRAJ, HD))]
    tables = (q_gain[None], k_gain[None], cos_tab, sin_tab)
    kept = [(width, HD, bf16), (TRAJ, HD, bf16), (TRAJ, HD, bf16), (width, HD, f32)]
    q_rot, k_rot, value, probs, mixed_own, mixed_other = by_trajectory(
        attend_kernel,
        kept + [(TRAJ, half, bf16)] * 2,
        [(TRAJ, wide)] * 2 + shared,
    )(flag, proj_own, proj_other, *tables)

    part_out = call(expand_kernel, [(flat, bf16)] * NX, 2 + 2 * NY, scalars=0)(
        mixed_own, mixed_other, *o_own, *o_other
    )
    part_out = [part_out[0]] + [take_x(part_out[k], -k) for k in range(1, NX)]
    out_rows = call(out_kernel, [(flat, bf16)], 2 + NX)(place, rows_own, *part_out)[0]

    gm_own, gm_other = call(
        project_kernel, [((tokens, half), bf16)] * 2, 1 + 2 * NY, scalars=0
    )(grad_all, *o_own, *o_other)
    g_own, g_other = by_trajectory(
        attend_back_kernel,
        [(TRAJ, wide, bf16)] * 2,
        [(TRAJ, wide)] * 2 + shared + [entry[:2] for entry in kept] + [(TRAJ, half)] * 2,
    )(flag, proj_own, proj_other, *tables, q_rot, k_rot, value, probs, gm_own, gm_other)

    span = NZ * HD
    *go_own, go_cross = call(
        weight_grad_kernel,
        [((span, half), bf16)] * NY + [((NY * span, half), bf16)],
        3,
        scalars=0,
    )(grad_all, mixed_own, mixed_other)
    *gw_own, gw_cross = call(
        weight_grad_kernel,
        [((span, wide), bf16)] * NY + [((NY * span, wide), bf16)],
        3,
        scalars=0,
    )(normed, g_own, g_other)

    back = call(expand_kernel, [(flat, bf16)] * NX, 2 + 2 * NY, scalars=0)(
        g_own, g_other, *qkv_own, *qkv_other
    )
    back = [back[0]] + [take_x(back[k], -k) for k in range(1, NX)]
    grad_rows = call(
        grad_rows_kernel, [(flat, bf16)], 5 + NX, scratch_shapes=[pltpu.VMEM(flat, f32)]
    )(place, rows_own, gain, cot_own, weight, *back)[0]

    go_mine, go_theirs = sum_weight(go_own, go_cross, at_owner, x, role)
    gw_mine, gw_theirs = sum_weight(gw_own, gw_cross, at_owner, x, role)
    gw_0, gw_1 = jnp.where(first, gw_mine, gw_theirs), jnp.where(first, gw_theirs, gw_mine)
    go_0, go_1 = jnp.where(first, go_mine, go_theirs), jnp.where(first, go_theirs, go_mine)

    def pick(value, item, lo, hi):
        return value[item * HD : (item + 1) * HD, lo:hi].astype(f32)

    grad_w_q = jnp.concatenate(
        [pick(gw, item, 0, half) for item in range(2) for gw in (gw_0, gw_1)], axis=1
    )
    grad_w_k = jnp.concatenate([pick(gw_0, item, half, half + HD) for item in range(2)], axis=1)
    grad_w_v = jnp.concatenate([pick(gw_1, item, half, half + HD) for item in range(2)], axis=1)
    grad_w_o = jnp.concatenate(
        [pick(go, item, 0, half).T for item in range(2) for go in (go_0, go_1)], axis=0
    )
    return (out_rows[None], grad_rows[None], grad_w_q, grad_w_k, grad_w_v, grad_w_o)


def solution(mesh):
    in_specs = (
        P(("dp", "fsdp"), "role", None),
        P(("dp", "fsdp"), "role", None),
        P(("dp", "fsdp"), "role"),
        P(("dp", "fsdp"), "role"),
        P(),
        P(),
        P(),
        P("fsdp", "role"),
        P("fsdp", "role"),
        P("fsdp", "role"),
        P("role", "fsdp"),
    )
    out_specs = (
        P(("dp", "fsdp"), "role", None),
        P(("dp", "fsdp"), "role", None),
        P("fsdp", "role"),
        P("fsdp", "role"),
        P("fsdp", "role"),
        P("role", "fsdp"),
    )
    return jax.shard_map(
        on_device, mesh=mesh, in_specs=in_specs, out_specs=out_specs, check_vma=False
    )
```

```python
import jax
import jax.numpy as jnp
from jax import lax
from jax.experimental import pallas as pl
from jax.experimental.pallas import tpu as pltpu
from jax.sharding import PartitionSpec as P

HD = 128
TRAJ = 128
NX = 4
NC = 2
NY = 4
NZ = 4

eps_norm = 1e-06
theta_base = 1000000.0
f32 = jnp.float32
bf16 = jnp.bfloat16


def dims(a, b, left, right):
    return lax.dot_general(left, right, (((a,), (b,)), ((), ())), preferred_element_type=f32)


def dot(left, right):
    return dims(1, 0, left, right)


def dot_rows(left, right):
    return dims(1, 1, left, right)


def dot_cols(left, right):
    return dims(0, 0, left, right)


def call(kernel, outs, vmem, scalars=1, **more):
    return pl.pallas_call(
        kernel,
        out_shape=[jax.ShapeDtypeStruct(shape, kind) for shape, kind in outs],
        in_specs=[pl.BlockSpec(memory_space=pltpu.SMEM)] * scalars
        + [pl.BlockSpec(memory_space=pltpu.VMEM)] * (vmem - scalars),
        out_specs=[pl.BlockSpec(memory_space=pltpu.VMEM)] * len(outs),
        compiler_params=pltpu.CompilerParams(vmem_limit_bytes=40 << 20),
        **more,
    )


def turned(place_ref, j):
    row = lax.rem(place_ref[0] + j // NZ, NY)
    col = lax.rem(place_ref[1] + j % NZ, NZ)
    return pl.ds(pl.multiple_of((row * NZ + col) * HD, HD), HD)


def norm_kernel(place_ref, rows_ref, gain_ref, normed_ref):
    x = rows_ref[...].astype(f32)
    inv = lax.rsqrt(jnp.mean(x * x, axis=-1, keepdims=True) + eps_norm)
    for j in range(NY * NZ):
        at = turned(place_ref, j)
        normed_ref[:, j * HD : (j + 1) * HD] = (
            rows_ref[:, at].astype(f32) * inv * gain_ref[:, at]
        ).astype(bf16)


def weigh_kernel(place_ref, cot_ref, weight_ref, grad_ref):
    weight = weight_ref[...]
    for j in range(NY * NZ):
        at = turned(place_ref, j)
        grad_ref[:, j * HD : (j + 1) * HD] = (cot_ref[:, at].astype(f32) * weight).astype(bf16)


def total_block(parts, j):
    cols = slice(j * HD, (j + 1) * HD)
    total = parts[0][:, cols].astype(f32)
    for part in parts[1:]:
        total = total + part[:, cols].astype(f32)
    return total


def finish_kernel(place_ref, rows_ref, gain_ref, cot_ref, weight_ref, *refs):
    outs, backs, (out_ref, grad_ref, scaled_ref) = refs[:NX], refs[NX : 2 * NX], refs[2 * NX :]
    for j in range(NY * NZ):
        at = turned(place_ref, j)
        out, back = total_block(outs, j), total_block(backs, j)
        out_ref[:, at] = (rows_ref[:, at].astype(f32) + out).astype(bf16)
        scaled_ref[:, at] = back * gain_ref[:, at]
    x = rows_ref[...].astype(f32)
    inv = lax.rsqrt(jnp.mean(x * x, axis=-1, keepdims=True) + eps_norm)
    scaled = scaled_ref[...]
    unit = x * inv
    mean = jnp.mean(scaled * unit, axis=-1, keepdims=True)
    grad_out = (cot_ref[...].astype(f32) * weight_ref[...]).astype(bf16).astype(f32)
    grad_ref[...] = (grad_out + inv * (scaled - unit * mean)).astype(bf16)


def project_kernel(normed_ref, *refs):
    own, other, outs = refs[:NY], refs[NY : 2 * NY], refs[2 * NY :]
    for chunks, out_ref in zip((own, other), outs):
        total = None
        for j in range(NY):
            span = chunks[j].shape[0]
            term = dot(normed_ref[:, j * span : (j + 1) * span], chunks[j][...])
            total = term if total is None else total + term
        out_ref[...] = total.astype(out_ref.dtype)


def expand_kernel(mixed_own_ref, mixed_other_ref, g_own_ref, g_other_ref, *refs):
    lefts = ((mixed_own_ref, mixed_other_ref), (g_own_ref, g_other_ref))
    outs = refs[4 * NY :]
    for part, (left_own_ref, left_other_ref) in enumerate(lefts):
        own = refs[2 * part * NY : (2 * part + 1) * NY]
        other = refs[(2 * part + 1) * NY : (2 * part + 2) * NY]
        for j in range(NY):
            span = own[j].shape[0]
            total = dot_rows(left_own_ref[...], own[j][...])
            total = total + dot_rows(left_other_ref[...], other[j][...])
            for k in range(NX):
                outs[part * NX + k][:, j * span : (j + 1) * span] = total[
                    k * TRAJ : (k + 1) * TRAJ
                ].astype(bf16)


def rotate(t, cos, sin):
    return t * cos + pltpu.roll(t, HD // 2, 1) * sin


def rotate_back(g, cos, sin):
    return g * cos + pltpu.roll(g * sin, HD // 2, 1)


def inv_norm(t):
    return lax.rsqrt(jnp.mean(t * t, axis=-1, keepdims=True) + eps_norm)


def norm_back(t, grad, gain):
    r = inv_norm(t)
    u = grad * gain
    return r * u - t * (r * r * r * jnp.mean(t * u, axis=-1, keepdims=True))


def stack_heads(own_ref, other_ref):
    return jnp.concatenate(
        [ref[:, k * HD : (k + 1) * HD] for ref in (own_ref, other_ref) for k in range(2)], axis=0
    )


def attend_kernel(
    first_ref, own_ref, other_ref, q_gain_ref, k_gain_ref, cos_ref, sin_ref,
    q_rot_ref, k_rot_ref, value_ref, probs_ref, mixed_own_ref, mixed_other_ref,
):
    cos, sin = cos_ref[...], sin_ref[...]
    cos4, sin4 = jnp.concatenate([cos] * 4, axis=0), jnp.concatenate([sin] * 4, axis=0)
    first = first_ref[0] == 1
    tail_own, tail_other = own_ref[:, 2 * HD :], other_ref[:, 2 * HD :]
    keys = jnp.where(first, tail_own, tail_other)
    value = jnp.where(first, tail_other, tail_own).astype(bf16)
    query = stack_heads(own_ref, other_ref)
    q_rot = rotate(query * inv_norm(query) * q_gain_ref[...], cos4, sin4).astype(bf16)
    k_rot = rotate(keys * inv_norm(keys) * k_gain_ref[...], cos, sin).astype(bf16)
    scores = dot_rows(q_rot, k_rot) * HD ** (-0.5)
    row = lax.broadcasted_iota(jnp.int32, scores.shape, 0) % TRAJ
    allowed = row >= lax.broadcasted_iota(jnp.int32, scores.shape, 1)
    scores = jnp.where(allowed, scores, -1e30)
    peak = jnp.max(scores, axis=-1, keepdims=True)
    weights = jnp.where(allowed, jnp.exp(scores - peak), 0.0)
    probs = weights / jnp.sum(weights, axis=-1, keepdims=True)
    mixed = dot(probs.astype(bf16), value).astype(bf16)
    q_rot_ref[...] = q_rot
    k_rot_ref[...] = k_rot
    value_ref[...] = value
    probs_ref[...] = probs
    for k in range(2):
        mixed_own_ref[:, k * HD : (k + 1) * HD] = mixed[k * TRAJ : (k + 1) * TRAJ]
        mixed_other_ref[:, k * HD : (k + 1) * HD] = mixed[(k + 2) * TRAJ : (k + 3) * TRAJ]


def attend_back_kernel(
    first_ref, own_ref, other_ref, q_gain_ref, k_gain_ref, cos_ref, sin_ref,
    q_rot_ref, k_rot_ref, value_ref, probs_ref, gm_own_ref, gm_other_ref,
    g_own_ref, g_other_ref,
):
    cos, sin = cos_ref[...], sin_ref[...]
    cos4, sin4 = jnp.concatenate([cos] * 4, axis=0), jnp.concatenate([sin] * 4, axis=0)
    first = first_ref[0] == 1
    keys = jnp.where(first, own_ref[:, 2 * HD :], other_ref[:, 2 * HD :])
    query = stack_heads(own_ref, other_ref)
    grad_mixed = stack_heads(gm_own_ref, gm_other_ref)
    q_rot, k_rot, value, probs = q_rot_ref[...], k_rot_ref[...], value_ref[...], probs_ref[...]
    grad_probs = dot_rows(grad_mixed, value)
    grad_value = dot_cols(probs.astype(bf16), grad_mixed).astype(bf16)
    inner = jnp.sum(grad_probs * probs, axis=-1, keepdims=True)
    grad_scores = (probs * (grad_probs - inner) * HD ** (-0.5)).astype(bf16)
    grad_q_rot = dot(grad_scores, k_rot)
    grad_k_rot = dot_cols(grad_scores, q_rot)
    grad_query = norm_back(query, rotate_back(grad_q_rot, cos4, sin4), q_gain_ref[...]).astype(bf16)
    grad_keys = norm_back(keys, rotate_back(grad_k_rot, cos, sin), k_gain_ref[...]).astype(bf16)
    for k in range(2):
        g_own_ref[:, k * HD : (k + 1) * HD] = grad_query[k * TRAJ : (k + 1) * TRAJ]
        g_other_ref[:, k * HD : (k + 1) * HD] = grad_query[(k + 2) * TRAJ : (k + 3) * TRAJ]
    g_own_ref[:, 2 * HD :] = jnp.where(first, grad_keys, grad_value)
    g_other_ref[:, 2 * HD :] = jnp.where(first, grad_value, grad_keys)


def by_trajectory(kernel, outs, ins):
    def spec(rows, cols):
        if rows == 0:
            return pl.BlockSpec(cols, lambda i: (0, 0))
        return pl.BlockSpec((rows, cols), lambda i: (i, 0))

    return pl.pallas_call(
        kernel,
        grid=(NX,),
        out_shape=[jax.ShapeDtypeStruct((rows * NX, cols), kind) for rows, cols, kind in outs],
        in_specs=[pl.BlockSpec(memory_space=pltpu.SMEM)] + [spec(*entry) for entry in ins],
        out_specs=[spec(rows, cols) for rows, cols, _ in outs],
        compiler_params=pltpu.CompilerParams(vmem_limit_bytes=40 << 20),
    )


def weight_grad_kernel(left_ref, own_ref, other_ref, *refs):
    outs, other_out = refs[:NY], refs[NY]
    for j in range(NY):
        span = outs[j].shape[0]
        left = left_ref[:, j * span : (j + 1) * span]
        other_out[j * span : (j + 1) * span] = dot_cols(left, other_ref[...]).astype(bf16)
        outs[j][...] = dot_cols(left, own_ref[...]).astype(bf16)


def rope_tables():
    position = jnp.arange(TRAJ, dtype=jnp.int32).astype(f32)
    inverse = jnp.exp(
        jnp.arange(HD // 2, dtype=f32) * (-2.0 * jnp.log(jnp.float32(theta_base)) / HD)
    )
    angles = position[:, None] * inverse[None, :]
    cos, sin = jnp.cos(angles), jnp.sin(angles)
    return jnp.concatenate([cos, cos], axis=1), jnp.concatenate([-sin, sin], axis=1)


def after(values, *earlier):
    alone = not isinstance(values, (list, tuple))
    values = (values,) if alone else tuple(values)
    held = lax.optimization_barrier(values + earlier)[: len(values)]
    return held[0] if alone else list(held)


def take_x(value, step):
    pairs = [
        (x * NC + c, (x - step) % NX * NC + c) for x in range(NX) for c in range(NC)
    ]
    return lax.ppermute(value, "dp", pairs)


def take_y(value, step):
    pairs = [(y * NZ + z, (y - step) % NY * NZ + z) for y in range(NY) for z in range(NZ)]
    return lax.ppermute(value, "fsdp", pairs)


def take_z(value, step):
    pairs = [(y * NZ + z, y * NZ + (z - step) % NZ) for y in range(NY) for z in range(NZ)]
    return lax.ppermute(value, "fsdp", pairs)


def other_core(value):
    return lax.ppermute(value, "dp", [(i, i ^ 1) for i in range(NX * NC)])


def owner_role(x):
    return x // (NX // 2)


def from_owner(value):
    n = NX * NC
    pairs = [(owner_role(d // NC) * n + d, (1 - owner_role(d // NC)) * n + d) for d in range(n)]
    return lax.ppermute(value, ("role", "dp"), pairs)


def to_owner(value):
    n = NX * NC
    pairs = [((1 - owner_role(d // NC)) * n + d, owner_role(d // NC) * n + d) for d in range(n)]
    return lax.ppermute(value, ("role", "dp"), pairs)


def spread_x(value, step):
    n = NX * NC
    pairs = [
        (owner_role(x) * n + x * NC + c, owner_role(x) * n + (x - step) % NX * NC + c)
        for x in range(NX)
        for c in range(NC)
    ]
    return lax.ppermute(value, ("role", "dp"), pairs)


def over_role(block, at_owner):
    return jnp.where(at_owner, block, from_owner(block))


def over_z(block):
    return jnp.concatenate([block] + [take_z(block, k) for k in range(1, NZ)], axis=0)


def over_y(plane):
    return [plane] + [take_y(plane, k) for k in range(1, NY)]


def over_x(value, *earlier):
    near = [take_x(value, 1), take_x(value, 3)]
    return [value, near[0], take_x(after(value, *near, *earlier), 2), near[1]], near


def add_core(own, theirs):
    span = own[0].shape[0]
    return [
        (own[k].astype(f32) + theirs[k * span : (k + 1) * span].astype(f32)).astype(bf16)
        for k in range(NY)
    ]


def add_y(terms, near):
    total = terms[0].astype(f32)
    for term in near + [take_y(terms[2], -2)]:
        total = total + term.astype(f32)
    span = total.shape[0] // NZ
    return [total[k * span : (k + 1) * span].astype(bf16) for k in range(NZ)]


def add_z(terms):
    total = terms[0].astype(f32)
    for k in range(1, NZ):
        total = total + take_z(terms[k], -k).astype(f32)
    return total.astype(bf16)


def add_role(term):
    return (term.astype(f32) + to_owner(term).astype(f32)).astype(bf16)


def share(total, x, role, *earlier):
    copies = [total] + after([spread_x(total, k) for k in range(1, NX)], *earlier)
    items = []
    for sub in range(2):
        source = role * 2 + sub
        item = copies[0]
        for k in range(1, NX):
            item = jnp.where((source - x) % NX == k, copies[k], item)
        items.append(item)
    mine = jnp.concatenate(items, axis=0)
    return mine, other_core(mine)


def on_device(rows, cotangent, advantage, action, norm_gain, q_gain, k_gain, w_q, w_k, w_v, w_o):
    role = lax.axis_index("role")
    dp = lax.axis_index("dp")
    fsdp = lax.axis_index("fsdp")
    x, core = dp // NC, dp % NC
    y, z = fsdp // NZ, fsdp % NZ
    at_owner = role == owner_role(x)
    sub = x % 2
    width = 4 * HD
    half = 2 * HD
    first = core == 0
    place = jnp.stack([y, z]).astype(jnp.int32)
    flag = first.astype(jnp.int32)[None]

    q_part = lax.dynamic_slice(w_q, (0, sub * width + core * half), (HD, half))
    k_part = lax.dynamic_slice(w_k, (0, sub * HD), (HD, HD))
    v_part = lax.dynamic_slice(w_v, (0, sub * HD), (HD, HD))
    qkv_block = jnp.concatenate([q_part, jnp.where(first, k_part, v_part)], axis=1)
    o_block = lax.dynamic_slice(w_o, (sub * width + core * half, 0), (half, HD)).T
    qkv_block = over_role(qkv_block, at_owner)
    o_block = over_role(after(o_block, qkv_block), at_owner)
    qkv_plane = over_z(qkv_block)

    rows_own, cot_own = rows[0], cotangent[0]
    gain = norm_gain[None]
    weight = (advantage[0] * action[0].astype(f32))[:, None]
    flat = (TRAJ, rows_own.shape[1])
    normed_own = call(norm_kernel, [(flat, bf16)], 3)(place, rows_own, gain)[0]
    normed_parts, _ = over_x(normed_own, qkv_plane)
    grad_turned = call(weigh_kernel, [(flat, bf16)], 3)(place, cot_own, weight)[0]
    grad_parts, grad_near = over_x(after(grad_turned, *normed_parts))

    qkv_own = over_y(qkv_plane)
    qkv_other = [other_core(piece) for piece in qkv_own]
    o_plane = over_z(after(o_block, qkv_own[1], qkv_own[3]))
    o_plane = after(o_plane, *qkv_own)
    o_own = over_y(o_plane)
    normed = after(jnp.concatenate(normed_parts, axis=0), *grad_near)
    grad_all = jnp.concatenate(grad_parts, axis=0)

    tokens = normed.shape[0]
    wide = half + HD
    cos_tab, sin_tab = rope_tables()
    proj_own, proj_other = call(
        project_kernel, [((tokens, wide), f32)] * 2, 1 + 2 * NY, scalars=0
    )(normed, *qkv_own, *qkv_other)
    o_late = after(o_own, proj_own)
    proj_own, proj_other = after([proj_own, proj_other], *o_own)
    o_own = o_late
    o_other = [other_core(piece) for piece in o_own]
    shared = [(0, (1, HD)), (0, (1, HD)), (0, (TRAJ, HD)), (0, (TRAJ, HD))]
    tables = (q_gain[None], k_gain[None], cos_tab, sin_tab)
    kept = [(width, HD, bf16), (TRAJ, HD, bf16), (TRAJ, HD, bf16), (width, HD, f32)]
    q_rot, k_rot, value, probs, mixed_own, mixed_other = by_trajectory(
        attend_kernel,
        kept + [(TRAJ, half, bf16)] * 2,
        [(TRAJ, wide)] * 2 + shared,
    )(flag, proj_own, proj_other, *tables)

    span = NZ * HD
    *go_own, go_cross = call(
        weight_grad_kernel,
        [((span, half), bf16)] * NY + [((NY * span, half), bf16)],
        3,
        scalars=0,
    )(grad_all, mixed_own, mixed_other)
    go_theirs = other_core(go_cross)
    go_terms = after(add_core(go_own, go_theirs), *o_own)

    gm_own, gm_other = call(
        project_kernel, [((tokens, half), bf16)] * 2, 1 + 2 * NY, scalars=0
    )(after(grad_all, go_cross), *o_own, *o_other)
    g_own, g_other = by_trajectory(
        attend_back_kernel,
        [(TRAJ, wide, bf16)] * 2,
        [(TRAJ, wide)] * 2 + shared + [entry[:2] for entry in kept] + [(TRAJ, half)] * 2,
    )(flag, proj_own, proj_other, *tables, q_rot, k_rot, value, probs, gm_own, gm_other)
    *gw_own, gw_cross = call(
        weight_grad_kernel,
        [((span, wide), bf16)] * NY + [((NY * span, wide), bf16)],
        3,
        scalars=0,
    )(normed, *after([g_own, g_other], go_theirs))
    gw_theirs = other_core(gw_cross)

    both = call(expand_kernel, [(flat, bf16)] * (2 * NX), 4 + 4 * NY, scalars=0)(
        mixed_own,
        mixed_other,
        *after([g_own, g_other], gw_cross),
        *o_own,
        *o_other,
        *qkv_own,
        *qkv_other,
    )
    gw_terms = add_core(gw_own, gw_theirs)
    both = after(both, gw_theirs)
    outs, backs = both[:NX], both[NX:]

    go_near = [take_y(go_terms[1], -1), take_y(go_terms[3], -3)]
    go_terms = add_y(go_terms, go_near)
    gw_terms = after(gw_terms, both[0], *go_near)
    gw_near = [take_y(gw_terms[1], -1), take_y(gw_terms[3], -3)]
    gw_terms = add_y(gw_terms, gw_near)
    out_near = [take_x(outs[1], -1), take_x(outs[3], -3)]
    go_term = add_z(after(go_terms, *gw_near, *out_near))
    backs = after(backs, *out_near)
    back_near = [take_x(backs[1], -1), take_x(backs[3], -3)]
    gw_term = add_z(after(gw_terms, *back_near))
    out_far = take_x(after(outs[2], *back_near), -2)
    back_far = take_x(after(backs[2], *back_near), -2)
    out_rows, grad_rows = call(
        finish_kernel, [(flat, bf16)] * 2, 5 + 2 * NX, scratch_shapes=[pltpu.VMEM(flat, f32)]
    )(
        place, rows_own, gain, cot_own, weight,
        outs[0], out_near[0], out_far, out_near[1],
        backs[0], back_near[0], back_far, back_near[1],
    )
    total = add_role(jnp.concatenate([gw_term, go_term], axis=1))
    mine, theirs = share(after(total, out_far, back_far), x, role, grad_rows)
    g_0, g_1 = jnp.where(first, mine, theirs), jnp.where(first, theirs, mine)

    def pick(value, item, lo, hi):
        return value[item * HD : (item + 1) * HD, lo:hi].astype(f32)

    grad_w_q = jnp.concatenate(
        [pick(g, item, 0, half) for item in range(2) for g in (g_0, g_1)], axis=1
    )
    grad_w_k = jnp.concatenate([pick(g_0, item, half, wide) for item in range(2)], axis=1)
    grad_w_v = jnp.concatenate([pick(g_1, item, half, wide) for item in range(2)], axis=1)
    grad_w_o = jnp.concatenate(
        [pick(g, item, wide, wide + half).T for item in range(2) for g in (g_0, g_1)], axis=0
    )
    return (out_rows[None], grad_rows[None], grad_w_q, grad_w_k, grad_w_v, grad_w_o)


def solution(mesh):
    in_specs = (
        P(("dp", "fsdp"), "role", None),
        P(("dp", "fsdp"), "role", None),
        P(("dp", "fsdp"), "role"),
        P(("dp", "fsdp"), "role"),
        P(),
        P(),
        P(),
        P("fsdp", "role"),
        P("fsdp", "role"),
        P("fsdp", "role"),
        P("role", "fsdp"),
    )
    out_specs = (
        P(("dp", "fsdp"), "role", None),
        P(("dp", "fsdp"), "role", None),
        P("fsdp", "role"),
        P("fsdp", "role"),
        P("fsdp", "role"),
        P("role", "fsdp"),
    )
    return jax.shard_map(
        on_device, mesh=mesh, in_specs=in_specs, out_specs=out_specs, check_vma=False
    )
```

```python
import jax
import jax.numpy as jnp
from jax import lax
from jax.experimental import pallas as pl
from jax.experimental.pallas import tpu as pltpu
from jax.sharding import PartitionSpec as P

HD = 128
TRAJ = 128
NX = 4
NC = 2
NY = 4
NZ = 4

eps_norm = 1e-06
theta_base = 1000000.0
f32 = jnp.float32
bf16 = jnp.bfloat16


def dims(a, b, left, right):
    return lax.dot_general(left, right, (((a,), (b,)), ((), ())), preferred_element_type=f32)


def dot(left, right):
    return dims(1, 0, left, right)


def dot_rows(left, right):
    return dims(1, 1, left, right)


def dot_cols(left, right):
    return dims(0, 0, left, right)


def call(kernel, outs, vmem, scalars=1, macs=0, **more):
    return pl.pallas_call(
        kernel,
        cost_estimate=pl.CostEstimate(
            flops=2 * macs,
            bytes_accessed=sum(shape[0] * shape[1] for shape, _ in outs) * 2,
            transcendentals=0,
        ),
        out_shape=[jax.ShapeDtypeStruct(shape, kind) for shape, kind in outs],
        in_specs=[pl.BlockSpec(memory_space=pltpu.SMEM)] * scalars
        + [pl.BlockSpec(memory_space=pltpu.VMEM)] * (vmem - scalars),
        out_specs=[pl.BlockSpec(memory_space=pltpu.VMEM)] * len(outs),
        compiler_params=pltpu.CompilerParams(vmem_limit_bytes=40 << 20),
        **more,
    )


def turned(place_ref, j):
    row = lax.rem(place_ref[0] + j // NZ, NY)
    col = lax.rem(place_ref[1] + j % NZ, NZ)
    return pl.ds(pl.multiple_of((row * NZ + col) * HD, HD), HD)


def norm_kernel(place_ref, rows_ref, gain_ref, normed_ref):
    x = rows_ref[...].astype(f32)
    inv = lax.rsqrt(jnp.mean(x * x, axis=-1, keepdims=True) + eps_norm)
    for j in range(NY * NZ):
        at = turned(place_ref, j)
        normed_ref[:, j * HD : (j + 1) * HD] = (
            rows_ref[:, at].astype(f32) * inv * gain_ref[:, at]
        ).astype(bf16)


def weigh_kernel(place_ref, cot_ref, weight_ref, grad_ref):
    weight = weight_ref[...]
    for j in range(NY * NZ):
        at = turned(place_ref, j)
        grad_ref[:, j * HD : (j + 1) * HD] = (cot_ref[:, at].astype(f32) * weight).astype(bf16)


def finish_kernel(
    place_ref, rows_ref, gain_ref, cot_ref, weight_ref, mixed_ref, back_ref, out_ref, grad_ref, scaled_ref
):
    for j in range(NY * NZ):
        at = turned(place_ref, j)
        cols = slice(j * HD, (j + 1) * HD)
        out_ref[:, at] = (rows_ref[:, at].astype(f32) + mixed_ref[:, cols].astype(f32)).astype(bf16)
        scaled_ref[:, at] = back_ref[:, cols].astype(f32) * gain_ref[:, at]
    x = rows_ref[...].astype(f32)
    inv = lax.rsqrt(jnp.mean(x * x, axis=-1, keepdims=True) + eps_norm)
    scaled = scaled_ref[...]
    unit = x * inv
    mean = jnp.mean(scaled * unit, axis=-1, keepdims=True)
    grad_out = (cot_ref[...].astype(f32) * weight_ref[...]).astype(bf16).astype(f32)
    grad_ref[...] = (grad_out + inv * (scaled - unit * mean)).astype(bf16)


def project_kernel(normed_ref, *refs):
    own, other, outs = refs[:NY], refs[NY : 2 * NY], refs[2 * NY :]
    for chunks, out_ref in zip((own, other), outs):
        total = None
        for j in range(NY):
            span = chunks[j].shape[0]
            term = dot(normed_ref[:, j * span : (j + 1) * span], chunks[j][...])
            total = term if total is None else total + term
        out_ref[...] = total.astype(out_ref.dtype)


def expand_kernel(left_own_ref, left_other_ref, *refs):
    own, other, out_ref = refs[:NY], refs[NY : 2 * NY], refs[2 * NY]
    for j in range(NY):
        span = own[j].shape[0]
        total = dot_rows(left_own_ref[...], own[j][...])
        total = total + dot_rows(left_other_ref[...], other[j][...])
        out_ref[:, j * span : (j + 1) * span] = total.astype(bf16)


def rotate(t, cos, sin):
    return t * cos + pltpu.roll(t, HD // 2, 1) * sin


def rotate_back(g, cos, sin):
    return g * cos + pltpu.roll(g * sin, HD // 2, 1)


def inv_norm(t):
    return lax.rsqrt(jnp.mean(t * t, axis=-1, keepdims=True) + eps_norm)


def norm_back(t, grad, gain):
    r = inv_norm(t)
    u = grad * gain
    return r * u - t * (r * r * r * jnp.mean(t * u, axis=-1, keepdims=True))


def stack_heads(own_ref, other_ref):
    return jnp.concatenate(
        [ref[:, k * HD : (k + 1) * HD] for ref in (own_ref, other_ref) for k in range(2)], axis=0
    )


def attend_kernel(
    first_ref, own_ref, other_ref, q_gain_ref, k_gain_ref, cos_ref, sin_ref,
    q_rot_ref, k_rot_ref, value_ref, probs_ref, mixed_own_ref, mixed_other_ref,
):
    cos, sin = cos_ref[...], sin_ref[...]
    cos4, sin4 = jnp.concatenate([cos] * 4, axis=0), jnp.concatenate([sin] * 4, axis=0)
    first = first_ref[0] == 1
    tail_own, tail_other = own_ref[:, 2 * HD :], other_ref[:, 2 * HD :]
    keys = jnp.where(first, tail_own, tail_other)
    value = jnp.where(first, tail_other, tail_own).astype(bf16)
    query = stack_heads(own_ref, other_ref)
    q_rot = rotate(query * inv_norm(query) * q_gain_ref[...], cos4, sin4).astype(bf16)
    k_rot = rotate(keys * inv_norm(keys) * k_gain_ref[...], cos, sin).astype(bf16)
    scores = dot_rows(q_rot, k_rot) * HD ** (-0.5)
    row = lax.broadcasted_iota(jnp.int32, scores.shape, 0) % TRAJ
    allowed = row >= lax.broadcasted_iota(jnp.int32, scores.shape, 1)
    scores = jnp.where(allowed, scores, -1e30)
    peak = jnp.max(scores, axis=-1, keepdims=True)
    weights = jnp.where(allowed, jnp.exp(scores - peak), 0.0)
    probs = weights / jnp.sum(weights, axis=-1, keepdims=True)
    mixed = dot(probs.astype(bf16), value).astype(bf16)
    q_rot_ref[...] = q_rot
    k_rot_ref[...] = k_rot
    value_ref[...] = value
    probs_ref[...] = probs
    for k in range(2):
        mixed_own_ref[:, k * HD : (k + 1) * HD] = mixed[k * TRAJ : (k + 1) * TRAJ]
        mixed_other_ref[:, k * HD : (k + 1) * HD] = mixed[(k + 2) * TRAJ : (k + 3) * TRAJ]


def attend_back_kernel(
    first_ref, own_ref, other_ref, q_gain_ref, k_gain_ref, cos_ref, sin_ref,
    q_rot_ref, k_rot_ref, value_ref, probs_ref, gm_own_ref, gm_other_ref,
    g_own_ref, g_other_ref,
):
    cos, sin = cos_ref[...], sin_ref[...]
    cos4, sin4 = jnp.concatenate([cos] * 4, axis=0), jnp.concatenate([sin] * 4, axis=0)
    first = first_ref[0] == 1
    keys = jnp.where(first, own_ref[:, 2 * HD :], other_ref[:, 2 * HD :])
    query = stack_heads(own_ref, other_ref)
    grad_mixed = stack_heads(gm_own_ref, gm_other_ref)
    q_rot, k_rot, value, probs = q_rot_ref[...], k_rot_ref[...], value_ref[...], probs_ref[...]
    grad_probs = dot_rows(grad_mixed, value)
    grad_value = dot_cols(probs.astype(bf16), grad_mixed).astype(bf16)
    inner = jnp.sum(grad_probs * probs, axis=-1, keepdims=True)
    grad_scores = (probs * (grad_probs - inner) * HD ** (-0.5)).astype(bf16)
    grad_q_rot = dot(grad_scores, k_rot)
    grad_k_rot = dot_cols(grad_scores, q_rot)
    grad_query = norm_back(query, rotate_back(grad_q_rot, cos4, sin4), q_gain_ref[...]).astype(bf16)
    grad_keys = norm_back(keys, rotate_back(grad_k_rot, cos, sin), k_gain_ref[...]).astype(bf16)
    for k in range(2):
        g_own_ref[:, k * HD : (k + 1) * HD] = grad_query[k * TRAJ : (k + 1) * TRAJ]
        g_other_ref[:, k * HD : (k + 1) * HD] = grad_query[(k + 2) * TRAJ : (k + 3) * TRAJ]
    g_own_ref[:, 2 * HD :] = jnp.where(first, grad_keys, grad_value)
    g_other_ref[:, 2 * HD :] = jnp.where(first, grad_value, grad_keys)


def by_trajectory(kernel, outs, ins):
    def spec(rows, cols):
        if rows == 0:
            return pl.BlockSpec(cols, lambda i: (0, 0))
        return pl.BlockSpec((rows, cols), lambda i: (i, 0))

    return pl.pallas_call(
        kernel,
        cost_estimate=pl.CostEstimate(
            flops=2 * 8 * NX * TRAJ * TRAJ * HD * 4, bytes_accessed=1 << 20, transcendentals=0
        ),
        grid=(NX,),
        out_shape=[jax.ShapeDtypeStruct((rows * NX, cols), kind) for rows, cols, kind in outs],
        in_specs=[pl.BlockSpec(memory_space=pltpu.SMEM)] + [spec(*entry) for entry in ins],
        out_specs=[spec(rows, cols) for rows, cols, _ in outs],
        compiler_params=pltpu.CompilerParams(vmem_limit_bytes=40 << 20),
    )


def weight_grad_kernel(left_ref, own_ref, other_ref, *refs):
    outs, other_out = refs[:NY], refs[NY]
    for j in range(NY):
        span = outs[j].shape[0]
        left = left_ref[:, j * span : (j + 1) * span]
        other_out[j * span : (j + 1) * span] = dot_cols(left, other_ref[...]).astype(bf16)
        outs[j][...] = dot_cols(left, own_ref[...]).astype(bf16)


def grad_o_kernel(place_ref, left_ref, own_ref, other_ref, own_out, other_out):
    span = NZ * HD
    for j in range(NY):
        left = left_ref[:, j * span : (j + 1) * span]
        at = pl.ds(pl.multiple_of(lax.rem(place_ref[0] + j, NY) * span, span), span)
        other_out[at] = dot_cols(left, other_ref[...]).astype(bf16)
        own_out[at] = dot_cols(left, own_ref[...]).astype(bf16)


def rope_tables():
    position = jnp.arange(TRAJ, dtype=jnp.int32).astype(f32)
    inverse = jnp.exp(
        jnp.arange(HD // 2, dtype=f32) * (-2.0 * jnp.log(jnp.float32(theta_base)) / HD)
    )
    angles = position[:, None] * inverse[None, :]
    cos, sin = jnp.cos(angles), jnp.sin(angles)
    return jnp.concatenate([cos, cos], axis=1), jnp.concatenate([-sin, sin], axis=1)


def after(values, *earlier):
    alone = not isinstance(values, (list, tuple))
    values = (values,) if alone else tuple(values)
    held = lax.optimization_barrier(values + earlier)[: len(values)]
    return held[0] if alone else list(held)


SAME_CORE = [[x * NC + c for x in range(NX)] for c in range(NC)]


def gather_x(value):
    return lax.all_gather(value, "dp", axis=0, tiled=True, axis_index_groups=SAME_CORE)


SAME_Z = [[y * NZ + z for y in range(NY)] for z in range(NZ)]


def scatter_y(value):
    return lax.psum_scatter(
        value, "fsdp", scatter_dimension=0, tiled=True, axis_index_groups=SAME_Z
    )


def scatter_x(value):
    return lax.psum_scatter(
        value, "dp", scatter_dimension=0, tiled=True, axis_index_groups=SAME_CORE
    )


def take_y(value, step):
    pairs = [(y * NZ + z, (y - step) % NY * NZ + z) for y in range(NY) for z in range(NZ)]
    return lax.ppermute(value, "fsdp", pairs)


def take_z(value, step):
    pairs = [(y * NZ + z, y * NZ + (z - step) % NZ) for y in range(NY) for z in range(NZ)]
    return lax.ppermute(value, "fsdp", pairs)


def other_core(value):
    return lax.ppermute(value, "dp", [(i, i ^ 1) for i in range(NX * NC)])


def owner_role(x):
    return x // (NX // 2)


def from_owner(value):
    n = NX * NC
    pairs = [(owner_role(d // NC) * n + d, (1 - owner_role(d // NC)) * n + d) for d in range(n)]
    return lax.ppermute(value, ("role", "dp"), pairs)


def to_owner(value):
    n = NX * NC
    pairs = [((1 - owner_role(d // NC)) * n + d, owner_role(d // NC) * n + d) for d in range(n)]
    return lax.ppermute(value, ("role", "dp"), pairs)


def spread_x(value, step):
    n = NX * NC
    pairs = [
        (owner_role(x) * n + x * NC + c, owner_role(x) * n + (x - step) % NX * NC + c)
        for x in range(NX)
        for c in range(NC)
    ]
    return lax.ppermute(value, ("role", "dp"), pairs)


def over_role(block, at_owner):
    return jnp.where(at_owner, block, from_owner(block))


def over_z(block):
    return jnp.concatenate([block] + [take_z(block, k) for k in range(1, NZ)], axis=0)


def over_y(plane):
    return [plane] + [take_y(plane, k) for k in range(1, NY)]


def add_core(own, theirs):
    span = own[0].shape[0]
    return [
        (own[k].astype(f32) + theirs[k * span : (k + 1) * span].astype(f32)).astype(bf16)
        for k in range(NY)
    ]


def add_y(terms):
    total = terms[0].astype(f32)
    for term in terms[1:]:
        total = total + term.astype(f32)
    span = total.shape[0] // NZ
    return [total[k * span : (k + 1) * span].astype(bf16) for k in range(NZ)]


def add_z(terms):
    total = terms[0].astype(f32)
    for k in range(1, NZ):
        total = total + take_z(terms[k], -k).astype(f32)
    return total.astype(bf16)


def add_role(term):
    return (term.astype(f32) + to_owner(term).astype(f32)).astype(bf16)


def share(total, x, role, *earlier):
    copies = [total] + after([spread_x(total, k) for k in range(1, NX)], *earlier)
    items = []
    for sub in range(2):
        source = role * 2 + sub
        item = copies[0]
        for k in range(1, NX):
            item = jnp.where((source - x) % NX == k, copies[k], item)
        items.append(item)
    mine = jnp.concatenate(items, axis=0)
    return mine, other_core(mine)


def on_device(rows, cotangent, advantage, action, norm_gain, q_gain, k_gain, w_q, w_k, w_v, w_o):
    role = lax.axis_index("role")
    dp = lax.axis_index("dp")
    fsdp = lax.axis_index("fsdp")
    x, core = dp // NC, dp % NC
    y, z = fsdp // NZ, fsdp % NZ
    at_owner = role == owner_role(x)
    sub = x % 2
    width = 4 * HD
    half = 2 * HD
    first = core == 0
    place = jnp.stack([y, z]).astype(jnp.int32)
    flag = first.astype(jnp.int32)[None]

    q_part = lax.dynamic_slice(w_q, (0, sub * width + core * half), (HD, half))
    k_part = lax.dynamic_slice(w_k, (0, sub * HD), (HD, HD))
    v_part = lax.dynamic_slice(w_v, (0, sub * HD), (HD, HD))
    o_part = lax.dynamic_slice(w_o, (sub * width + core * half, 0), (half, HD)).T
    wide = half + HD
    kv_part = jnp.where(first, k_part, v_part)
    block_part = jnp.concatenate([q_part, kv_part, o_part], axis=1)
    block = over_role(block_part, at_owner)
    qkv_plane = over_z(block[:, :wide])

    rows_own, cot_own = rows[0], cotangent[0]
    gain = norm_gain[None]
    weight = (advantage[0] * action[0].astype(f32))[:, None]
    flat = (TRAJ, rows_own.shape[1])
    normed_own = call(norm_kernel, [(flat, bf16)], 3)(place, after(rows_own, block_part), gain)[0]
    normed = gather_x(normed_own)
    cot_late = after(cot_own, block)
    grad_turned = call(weigh_kernel, [(flat, bf16)], 3)(place, cot_late, weight)[0]
    grad_all = gather_x(grad_turned)

    qkv_own = over_y(qkv_plane)
    qkv_first = other_core(qkv_plane)
    o_plane = over_z(after(block[:, wide:], qkv_first))
    o_first = other_core(o_plane)
    qkv_other = [qkv_first] + [other_core(after(piece, o_first)) for piece in qkv_own[1:]]
    o_late = after(o_plane, *qkv_own)
    o_near = [take_y(o_late, 1), take_y(o_late, 3)]

    tokens = normed.shape[0]
    cos_tab, sin_tab = rope_tables()
    proj_own, proj_other = call(
        project_kernel, [((tokens, wide), f32)] * 2, 1 + 2 * NY, scalars=0, macs=tokens * flat[1] * 2 * wide
    )(normed, *qkv_own, *qkv_other)
    o_own = [o_plane, o_near[0], take_y(after(o_plane, proj_own), 2), o_near[1]]
    o_other = [o_first] + [other_core(piece) for piece in o_own[1:]]
    proj_own, proj_other = after([proj_own, proj_other], *o_near)
    shared = [(0, (1, HD)), (0, (1, HD)), (0, (TRAJ, HD)), (0, (TRAJ, HD))]
    tables = (q_gain[None], k_gain[None], cos_tab, sin_tab)
    kept = [(width, HD, bf16), (TRAJ, HD, bf16), (TRAJ, HD, bf16), (width, HD, f32)]
    q_rot, k_rot, value, probs, mixed_own, mixed_other = by_trajectory(
        attend_kernel,
        kept + [(TRAJ, half, bf16)] * 2,
        [(TRAJ, wide)] * 2 + shared,
    )(flag, proj_own, proj_other, *tables)

    span = NZ * HD
    go_own, go_cross = call(
        grad_o_kernel, [((NY * span, half), bf16)] * 2, 4, macs=tokens * flat[1] * width
    )(place, after(grad_all, o_own[2], o_other[1], o_other[3]), mixed_own, mixed_other)
    gm_own, gm_other = call(
        project_kernel, [((tokens, half), bf16)] * 2, 1 + 2 * NY, scalars=0, macs=tokens * flat[1] * width
    )(after(grad_all, go_cross), *o_own, *o_other)
    go_theirs = after(other_core(go_cross), gm_own)
    go_terms = scatter_y((go_own.astype(f32) + go_theirs.astype(f32)).astype(bf16))
    g_own, g_other = by_trajectory(
        attend_back_kernel,
        [(TRAJ, wide, bf16)] * 2,
        [(TRAJ, wide)] * 2 + shared + [entry[:2] for entry in kept] + [(TRAJ, half)] * 2,
    )(flag, proj_own, proj_other, *tables, q_rot, k_rot, value, probs, *after([gm_own, gm_other], go_theirs))
    *gw_own, gw_cross = call(
        weight_grad_kernel,
        [((span, wide), bf16)] * NY + [((NY * span, wide), bf16)],
        3,
        scalars=0,
    )(normed, g_own, g_other)
    gw_theirs = other_core(gw_cross)
    spread = ((tokens, flat[1]), bf16)
    part_out = call(expand_kernel, [spread], 2 + 2 * NY, scalars=0, macs=tokens * flat[1] * width)(
        *after([mixed_own, mixed_other], gw_cross), *o_own, *o_other
    )[0]
    gw_terms = after(add_core(gw_own, gw_theirs), part_out)
    gw_near = [take_y(gw_terms[1], -1), take_y(gw_terms[3], -3)]
    back = call(expand_kernel, [spread], 2 + 2 * NY, scalars=0, macs=tokens * flat[1] * 2 * wide)(
        *after([g_own, g_other], *gw_near), *qkv_own, *qkv_other
    )[0]
    out_total = scatter_x(part_out)
    back_total = scatter_x(back)

    go_terms = after(go_terms, *gw_near)
    go_term = add_z([go_terms[k * HD : (k + 1) * HD] for k in range(NZ)])
    gw_far = take_y(after(gw_terms[2], *gw_near), -2)
    gw_terms = add_y([gw_terms[0], *gw_near, after(gw_far, go_term)])
    gw_term = add_z(gw_terms)
    out_rows, grad_rows = call(
        finish_kernel, [(flat, bf16)] * 2, 7, scratch_shapes=[pltpu.VMEM(flat, f32)]
    )(place, rows_own, gain, cot_own, weight, out_total, back_total)
    total = add_role(jnp.concatenate([gw_term, go_term], axis=1))
    mine, theirs = share(after(total, out_total), x, role, grad_rows)
    g_0, g_1 = jnp.where(first, mine, theirs), jnp.where(first, theirs, mine)

    def pick(value, item, lo, hi):
        return value[item * HD : (item + 1) * HD, lo:hi].astype(f32)

    grad_w_q = jnp.concatenate(
        [pick(g, item, 0, half) for item in range(2) for g in (g_0, g_1)], axis=1
    )
    grad_w_k = jnp.concatenate([pick(g_0, item, half, wide) for item in range(2)], axis=1)
    grad_w_v = jnp.concatenate([pick(g_1, item, half, wide) for item in range(2)], axis=1)
    grad_w_o = jnp.concatenate(
        [pick(g, item, wide, wide + half).T for item in range(2) for g in (g_0, g_1)], axis=0
    )
    return (out_rows[None], grad_rows[None], grad_w_q, grad_w_k, grad_w_v, grad_w_o)


def solution(mesh):
    in_specs = (
        P(("dp", "fsdp"), "role", None),
        P(("dp", "fsdp"), "role", None),
        P(("dp", "fsdp"), "role"),
        P(("dp", "fsdp"), "role"),
        P(),
        P(),
        P(),
        P("fsdp", "role"),
        P("fsdp", "role"),
        P("fsdp", "role"),
        P("role", "fsdp"),
    )
    out_specs = (
        P(("dp", "fsdp"), "role", None),
        P(("dp", "fsdp"), "role", None),
        P("fsdp", "role"),
        P("fsdp", "role"),
        P("fsdp", "role"),
        P("role", "fsdp"),
    )
    return jax.shard_map(
        on_device, mesh=mesh, in_specs=in_specs, out_specs=out_specs, check_vma=False
    )
```

```python
from functools import partial

import jax
import jax.numpy as jnp
from jax import lax
from jax.experimental import pallas as pl
from jax.experimental.pallas import tpu as pltpu
from jax.sharding import PartitionSpec as P

HD = 128
TRAJ = 128
NX = 4
NC = 2
NY = 4
NZ = 4

eps_norm = 1e-06
theta_base = 1000000.0
f32 = jnp.float32
bf16 = jnp.bfloat16


def dims(a, b, left, right):
    return lax.dot_general(left, right, (((a,), (b,)), ((), ())), preferred_element_type=f32)


def dot(left, right):
    return dims(1, 0, left, right)


def dot_rows(left, right):
    return dims(1, 1, left, right)


def dot_cols(left, right):
    return dims(0, 0, left, right)


def call(kernel, outs, vmem, scalars=1, macs=0, **more):
    return pl.pallas_call(
        kernel,
        cost_estimate=pl.CostEstimate(
            flops=2 * macs,
            bytes_accessed=sum(shape[0] * shape[1] for shape, _ in outs) * 2,
            transcendentals=0,
        ),
        out_shape=[jax.ShapeDtypeStruct(shape, kind) for shape, kind in outs],
        in_specs=[pl.BlockSpec(memory_space=pltpu.SMEM)] * scalars
        + [pl.BlockSpec(memory_space=pltpu.VMEM)] * (vmem - scalars),
        out_specs=[pl.BlockSpec(memory_space=pltpu.VMEM)] * len(outs),
        compiler_params=pltpu.CompilerParams(vmem_limit_bytes=16 << 20),
        **more,
    )


def turned(place_ref, j):
    row = lax.rem(place_ref[0] + j // NZ, NY)
    col = lax.rem(place_ref[1] + j % NZ, NZ)
    return pl.ds(pl.multiple_of((row * NZ + col) * HD, HD), HD)


def rows_kernel(place_ref, rows_ref, gain_ref, cot_ref, weight_ref, out_ref):
    x = rows_ref[...].astype(f32)
    inv = lax.rsqrt(jnp.mean(x * x, axis=-1, keepdims=True) + eps_norm)
    weight = weight_ref[...]
    for j in range(NY * NZ):
        at = turned(place_ref, j)
        cols = slice(j * HD, (j + 1) * HD)
        out_ref[:TRAJ, cols] = (rows_ref[:, at].astype(f32) * inv * gain_ref[:, at]).astype(bf16)
        out_ref[TRAJ:, cols] = (cot_ref[:, at].astype(f32) * weight).astype(bf16)


def tokens_of(pair_ref, part, cols):
    tops = [(2 * k + part) * TRAJ for k in range(NX)]
    return jnp.concatenate([pair_ref[top : top + TRAJ, cols] for top in tops], axis=0)


def finish_kernel(
    place_ref, rows_ref, gain_ref, cot_ref, weight_ref, total_ref, out_ref, grad_ref, scaled_ref
):
    for j in range(NY * NZ):
        at = turned(place_ref, j)
        cols = slice(j * HD, (j + 1) * HD)
        mixed, back = total_ref[:TRAJ, cols].astype(f32), total_ref[TRAJ:, cols].astype(f32)
        out_ref[:, at] = (rows_ref[:, at].astype(f32) + mixed).astype(bf16)
        scaled_ref[:, at] = back * gain_ref[:, at]
    x = rows_ref[...].astype(f32)
    inv = lax.rsqrt(jnp.mean(x * x, axis=-1, keepdims=True) + eps_norm)
    scaled = scaled_ref[...]
    unit = x * inv
    mean = jnp.mean(scaled * unit, axis=-1, keepdims=True)
    grad_out = (cot_ref[...].astype(f32) * weight_ref[...]).astype(bf16).astype(f32)
    grad_ref[...] = (grad_out + inv * (scaled - unit * mean)).astype(bf16)


def project_kernel(part, pair_ref, *refs):
    own, other, outs = refs[:NY], refs[NY : 2 * NY], refs[2 * NY :]
    totals = [None, None]
    for j in range(NY):
        span = own[j].shape[0]
        left = tokens_of(pair_ref, part, slice(j * span, (j + 1) * span))
        for side, chunks in enumerate((own, other)):
            term = dot(left, chunks[j][...])
            totals[side] = term if totals[side] is None else totals[side] + term
    for out_ref, total in zip(outs, totals):
        out_ref[...] = total.astype(out_ref.dtype)


def expand_kernel(mixed_own_ref, mixed_other_ref, g_own_ref, g_other_ref, *refs):
    out_ref = refs[4 * NY]
    lefts = ((mixed_own_ref, mixed_other_ref), (g_own_ref, g_other_ref))
    for part, (left_own_ref, left_other_ref) in enumerate(lefts):
        own = refs[2 * part * NY : (2 * part + 1) * NY]
        other = refs[(2 * part + 1) * NY : (2 * part + 2) * NY]
        for j in range(NY):
            span = own[j].shape[0]
            total = dot_rows(left_own_ref[...], own[j][...])
            total = total + dot_rows(left_other_ref[...], other[j][...])
            for k in range(NX):
                top = (2 * k + part) * TRAJ
                out_ref[top : top + TRAJ, j * span : (j + 1) * span] = total[
                    k * TRAJ : (k + 1) * TRAJ
                ].astype(bf16)


def rotate(t, cos, sin):
    return t * cos + pltpu.roll(t, HD // 2, 1) * sin


def rotate_back(g, cos, sin):
    return g * cos + pltpu.roll(g * sin, HD // 2, 1)


def inv_norm(t):
    return lax.rsqrt(jnp.mean(t * t, axis=-1, keepdims=True) + eps_norm)


def norm_back(t, grad, gain):
    r = inv_norm(t)
    u = grad * gain
    return r * u - t * (r * r * r * jnp.mean(t * u, axis=-1, keepdims=True))


def stack_heads(own_ref, other_ref):
    return jnp.concatenate(
        [ref[:, k * HD : (k + 1) * HD] for ref in (own_ref, other_ref) for k in range(2)], axis=0
    )


def attend_kernel(
    first_ref, own_ref, other_ref, q_gain_ref, k_gain_ref, cos_ref, sin_ref,
    q_rot_ref, k_rot_ref, value_ref, probs_ref, mixed_own_ref, mixed_other_ref,
):
    cos, sin = cos_ref[...], sin_ref[...]
    cos4, sin4 = jnp.concatenate([cos] * 4, axis=0), jnp.concatenate([sin] * 4, axis=0)
    first = first_ref[0] == 1
    tail_own, tail_other = own_ref[:, 2 * HD :], other_ref[:, 2 * HD :]
    keys = jnp.where(first, tail_own, tail_other)
    value = jnp.where(first, tail_other, tail_own).astype(bf16)
    query = stack_heads(own_ref, other_ref)
    q_rot = rotate(query * inv_norm(query) * q_gain_ref[...], cos4, sin4).astype(bf16)
    k_rot = rotate(keys * inv_norm(keys) * k_gain_ref[...], cos, sin).astype(bf16)
    scores = dot_rows(q_rot, k_rot) * HD ** (-0.5)
    row = lax.broadcasted_iota(jnp.int32, scores.shape, 0) % TRAJ
    allowed = row >= lax.broadcasted_iota(jnp.int32, scores.shape, 1)
    scores = jnp.where(allowed, scores, -1e30)
    peak = jnp.max(scores, axis=-1, keepdims=True)
    weights = jnp.where(allowed, jnp.exp(scores - peak), 0.0)
    probs = weights / jnp.sum(weights, axis=-1, keepdims=True)
    mixed = dot(probs.astype(bf16), value).astype(bf16)
    q_rot_ref[...] = q_rot
    k_rot_ref[...] = k_rot
    value_ref[...] = value
    probs_ref[...] = probs
    for k in range(2):
        mixed_own_ref[:, k * HD : (k + 1) * HD] = mixed[k * TRAJ : (k + 1) * TRAJ]
        mixed_other_ref[:, k * HD : (k + 1) * HD] = mixed[(k + 2) * TRAJ : (k + 3) * TRAJ]


def attend_back_kernel(
    first_ref, own_ref, other_ref, q_gain_ref, k_gain_ref, cos_ref, sin_ref,
    q_rot_ref, k_rot_ref, value_ref, probs_ref, gm_own_ref, gm_other_ref,
    g_own_ref, g_other_ref,
):
    cos, sin = cos_ref[...], sin_ref[...]
    cos4, sin4 = jnp.concatenate([cos] * 4, axis=0), jnp.concatenate([sin] * 4, axis=0)
    first = first_ref[0] == 1
    keys = jnp.where(first, own_ref[:, 2 * HD :], other_ref[:, 2 * HD :])
    query = stack_heads(own_ref, other_ref)
    grad_mixed = stack_heads(gm_own_ref, gm_other_ref)
    q_rot, k_rot, value, probs = q_rot_ref[...], k_rot_ref[...], value_ref[...], probs_ref[...]
    grad_probs = dot_rows(grad_mixed, value)
    grad_value = dot_cols(probs.astype(bf16), grad_mixed).astype(bf16)
    inner = jnp.sum(grad_probs * probs, axis=-1, keepdims=True)
    grad_scores = (probs * (grad_probs - inner) * HD ** (-0.5)).astype(bf16)
    grad_q_rot = dot(grad_scores, k_rot)
    grad_k_rot = dot_cols(grad_scores, q_rot)
    grad_query = norm_back(query, rotate_back(grad_q_rot, cos4, sin4), q_gain_ref[...]).astype(bf16)
    grad_keys = norm_back(keys, rotate_back(grad_k_rot, cos, sin), k_gain_ref[...]).astype(bf16)
    for k in range(2):
        g_own_ref[:, k * HD : (k + 1) * HD] = grad_query[k * TRAJ : (k + 1) * TRAJ]
        g_other_ref[:, k * HD : (k + 1) * HD] = grad_query[(k + 2) * TRAJ : (k + 3) * TRAJ]
    g_own_ref[:, 2 * HD :] = jnp.where(first, grad_keys, grad_value)
    g_other_ref[:, 2 * HD :] = jnp.where(first, grad_value, grad_keys)


def by_trajectory(kernel, outs, ins):
    def spec(rows, cols):
        if rows == 0:
            return pl.BlockSpec(cols, lambda i: (0, 0))
        return pl.BlockSpec((rows, cols), lambda i: (i, 0))

    return pl.pallas_call(
        kernel,
        cost_estimate=pl.CostEstimate(
            flops=2 * 8 * NX * TRAJ * TRAJ * HD * 4, bytes_accessed=1 << 20, transcendentals=0
        ),
        grid=(NX,),
        out_shape=[jax.ShapeDtypeStruct((rows * NX, cols), kind) for rows, cols, kind in outs],
        in_specs=[pl.BlockSpec(memory_space=pltpu.SMEM)] + [spec(*entry) for entry in ins],
        out_specs=[spec(rows, cols) for rows, cols, _ in outs],
        compiler_params=pltpu.CompilerParams(vmem_limit_bytes=16 << 20),
    )


def weight_grad_kernel(pair_ref, own_ref, other_ref, *refs):
    outs, other_out = refs[:NY], refs[NY]
    for j in range(NY):
        span = outs[j].shape[0]
        left = tokens_of(pair_ref, 0, slice(j * span, (j + 1) * span))
        other_out[j * span : (j + 1) * span] = dot_cols(left, other_ref[...]).astype(bf16)
        outs[j][...] = dot_cols(left, own_ref[...]).astype(bf16)


def grad_o_kernel(place_ref, pair_ref, own_ref, other_ref, own_out, other_out):
    span = NZ * HD
    for j in range(NY):
        left = tokens_of(pair_ref, 1, slice(j * span, (j + 1) * span))
        at = pl.ds(pl.multiple_of(lax.rem(place_ref[0] + j, NY) * span, span), span)
        other_out[at] = dot_cols(left, other_ref[...]).astype(bf16)
        own_out[at] = dot_cols(left, own_ref[...]).astype(bf16)


def rope_tables():
    position = jnp.arange(TRAJ, dtype=jnp.int32).astype(f32)
    inverse = jnp.exp(
        jnp.arange(HD // 2, dtype=f32) * (-2.0 * jnp.log(jnp.float32(theta_base)) / HD)
    )
    angles = position[:, None] * inverse[None, :]
    cos, sin = jnp.cos(angles), jnp.sin(angles)
    return jnp.concatenate([cos, cos], axis=1), jnp.concatenate([-sin, sin], axis=1)


def after(values, *earlier):
    alone = not isinstance(values, (list, tuple))
    values = (values,) if alone else tuple(values)
    held = lax.optimization_barrier(values + earlier)[: len(values)]
    return held[0] if alone else list(held)


SAME_CORE = [[x * NC + c for x in range(NX)] for c in range(NC)]


def gather_x(value):
    return lax.all_gather(value, "dp", axis=0, tiled=True, axis_index_groups=SAME_CORE)


SAME_Z = [[y * NZ + z for y in range(NY)] for z in range(NZ)]


def scatter_y(value):
    return lax.psum_scatter(
        value, "fsdp", scatter_dimension=0, tiled=True, axis_index_groups=SAME_Z
    )


def scatter_x(value):
    return lax.psum_scatter(
        value, "dp", scatter_dimension=0, tiled=True, axis_index_groups=SAME_CORE
    )


def take_y(value, step):
    pairs = [(y * NZ + z, (y - step) % NY * NZ + z) for y in range(NY) for z in range(NZ)]
    return lax.ppermute(value, "fsdp", pairs)


def take_z(value, step):
    pairs = [(y * NZ + z, y * NZ + (z - step) % NZ) for y in range(NY) for z in range(NZ)]
    return lax.ppermute(value, "fsdp", pairs)


def other_core(value):
    return lax.ppermute(value, "dp", [(i, i ^ 1) for i in range(NX * NC)])


def owner_role(x):
    return x // (NX // 2)


def from_owner(value):
    n = NX * NC
    pairs = [(owner_role(d // NC) * n + d, (1 - owner_role(d // NC)) * n + d) for d in range(n)]
    return lax.ppermute(value, ("role", "dp"), pairs)


def to_owner(value):
    n = NX * NC
    pairs = [((1 - owner_role(d // NC)) * n + d, owner_role(d // NC) * n + d) for d in range(n)]
    return lax.ppermute(value, ("role", "dp"), pairs)


def spread_x(value, step):
    n = NX * NC
    pairs = [
        (owner_role(x) * n + x * NC + c, owner_role(x) * n + (x - step) % NX * NC + c)
        for x in range(NX)
        for c in range(NC)
    ]
    return lax.ppermute(value, ("role", "dp"), pairs)


def over_role(block, at_owner):
    return jnp.where(at_owner, block, from_owner(block))


def over_z(block):
    return jnp.concatenate([block] + [take_z(block, k) for k in range(1, NZ)], axis=0)


def over_y(plane):
    return [plane] + [take_y(plane, k) for k in range(1, NY)]


def add_core(own, theirs):
    span = own[0].shape[0]
    return [
        (own[k].astype(f32) + theirs[k * span : (k + 1) * span].astype(f32)).astype(bf16)
        for k in range(NY)
    ]


def add_y(terms):
    total = terms[0].astype(f32)
    for term in terms[1:]:
        total = total + term.astype(f32)
    span = total.shape[0] // NZ
    return [total[k * span : (k + 1) * span].astype(bf16) for k in range(NZ)]


def add_z(terms):
    total = terms[0].astype(f32)
    for k in range(1, NZ):
        total = total + take_z(terms[k], -k).astype(f32)
    return total.astype(bf16)


def add_role(term):
    return (term.astype(f32) + to_owner(term).astype(f32)).astype(bf16)


def share(total, x, role, *earlier):
    copies = [total] + after([spread_x(total, k) for k in range(1, NX)], *earlier)
    items = []
    for sub in range(2):
        source = role * 2 + sub
        item = copies[0]
        for k in range(1, NX):
            item = jnp.where((source - x) % NX == k, copies[k], item)
        items.append(item)
    mine = jnp.concatenate(items, axis=0)
    return mine, other_core(mine)


def on_device(rows, cotangent, advantage, action, norm_gain, q_gain, k_gain, w_q, w_k, w_v, w_o):
    role = lax.axis_index("role")
    dp = lax.axis_index("dp")
    fsdp = lax.axis_index("fsdp")
    x, core = dp // NC, dp % NC
    y, z = fsdp // NZ, fsdp % NZ
    at_owner = role == owner_role(x)
    sub = x % 2
    width = 4 * HD
    half = 2 * HD
    first = core == 0
    place = jnp.stack([y, z]).astype(jnp.int32)
    flag = first.astype(jnp.int32)[None]

    q_part = lax.dynamic_slice(w_q, (0, sub * width + core * half), (HD, half))
    k_part = lax.dynamic_slice(w_k, (0, sub * HD), (HD, HD))
    v_part = lax.dynamic_slice(w_v, (0, sub * HD), (HD, HD))
    o_part = lax.dynamic_slice(w_o, (sub * width + core * half, 0), (half, HD)).T
    wide = half + HD
    kv_part = jnp.where(first, k_part, v_part)
    block_part = jnp.concatenate([q_part, kv_part, o_part], axis=1)
    block = over_role(block_part, at_owner)
    qkv_plane = over_z(block[:, :wide])

    rows_own, cot_own = rows[0], cotangent[0]
    gain = norm_gain[None]
    weight = (advantage[0] * action[0].astype(f32))[:, None]
    flat = (TRAJ, rows_own.shape[1])
    pair_own = call(rows_kernel, [((2 * TRAJ, flat[1]), bf16)], 5)(
        place, after(rows_own, block_part), gain, cot_own, weight
    )[0]
    pair = gather_x(pair_own)

    qkv_own = over_y(qkv_plane)
    qkv_first = other_core(qkv_plane)
    o_plane = over_z(after(block[:, wide:], qkv_first))
    o_first = other_core(o_plane)
    qkv_other = [qkv_first] + [other_core(after(piece, o_first)) for piece in qkv_own[1:]]
    o_late = after(o_plane, *qkv_own)
    o_near = [take_y(o_late, 1), take_y(o_late, 3)]

    tokens = pair.shape[0] // 2
    cos_tab, sin_tab = rope_tables()
    proj_own, proj_other = call(
        partial(project_kernel, 0), [((tokens, wide), f32)] * 2, 1 + 2 * NY, scalars=0, macs=tokens * flat[1] * 2 * wide
    )(pair, *qkv_own, *qkv_other)
    o_own = [o_plane, o_near[0], take_y(after(o_plane, proj_own), 2), o_near[1]]
    o_other = [o_first] + [other_core(after(piece, proj_own)) for piece in o_own[1:]]
    proj_own, proj_other = after([proj_own, proj_other], *o_near)
    shared = [(0, (1, HD)), (0, (1, HD)), (0, (TRAJ, HD)), (0, (TRAJ, HD))]
    tables = (q_gain[None], k_gain[None], cos_tab, sin_tab)
    kept = [(width, HD, bf16), (TRAJ, HD, bf16), (TRAJ, HD, bf16), (width, HD, f32)]
    q_rot, k_rot, value, probs, mixed_own, mixed_other = by_trajectory(
        attend_kernel,
        kept + [(TRAJ, half, bf16)] * 2,
        [(TRAJ, wide)] * 2 + shared,
    )(flag, proj_own, proj_other, *tables)

    span = NZ * HD
    go_own, go_cross = call(
        grad_o_kernel, [((NY * span, half), bf16)] * 2, 4, macs=tokens * flat[1] * width
    )(place, after(pair, o_own[2], o_other[1], o_other[3]), mixed_own, mixed_other)
    gm_own, gm_other = call(
        partial(project_kernel, 1), [((tokens, half), bf16)] * 2, 1 + 2 * NY, scalars=0, macs=tokens * flat[1] * width
    )(after(pair, go_cross), *o_own, *o_other)
    go_theirs = after(other_core(go_cross), gm_own)
    go_terms = scatter_y((go_own.astype(f32) + go_theirs.astype(f32)).astype(bf16))
    g_own, g_other = by_trajectory(
        attend_back_kernel,
        [(TRAJ, wide, bf16)] * 2,
        [(TRAJ, wide)] * 2 + shared + [entry[:2] for entry in kept] + [(TRAJ, half)] * 2,
    )(flag, proj_own, proj_other, *tables, q_rot, k_rot, value, probs, *after([gm_own, gm_other], go_theirs))
    *gw_own, gw_cross = call(
        weight_grad_kernel,
        [((span, wide), bf16)] * NY + [((NY * span, wide), bf16)],
        3,
        scalars=0,
    )(pair, g_own, g_other)
    gw_theirs = other_core(gw_cross)
    terms = call(
        expand_kernel,
        [((2 * tokens, flat[1]), bf16)],
        4 + 4 * NY,
        scalars=0,
        macs=tokens * flat[1] * (width + 2 * wide),
    )(mixed_own, mixed_other, *after([g_own, g_other], gw_cross), *o_own, *o_other, *qkv_own, *qkv_other)[0]
    row_total = scatter_x(terms)

    gw_terms = after(add_core(gw_own, gw_theirs), terms)
    gw_near = [take_y(gw_terms[1], -1), take_y(gw_terms[3], -3)]
    go_terms = after(go_terms, *gw_near)
    go_term = add_z([go_terms[k * HD : (k + 1) * HD] for k in range(NZ)])
    gw_far = take_y(after(gw_terms[2], *gw_near), -2)
    gw_terms = add_y([gw_terms[0], *gw_near, after(gw_far, go_term)])
    gw_term = add_z(gw_terms)
    out_rows, grad_rows = call(
        finish_kernel, [(flat, bf16)] * 2, 6, scratch_shapes=[pltpu.VMEM(flat, f32)]
    )(place, rows_own, gain, cot_own, weight, row_total)
    total = add_role(jnp.concatenate([gw_term, go_term], axis=1))
    mine, theirs = share(total, x, role, grad_rows)
    g_0, g_1 = jnp.where(first, mine, theirs), jnp.where(first, theirs, mine)

    def pick(value, item, lo, hi):
        return value[item * HD : (item + 1) * HD, lo:hi].astype(f32)

    grad_w_q = jnp.concatenate(
        [pick(g, item, 0, half) for item in range(2) for g in (g_0, g_1)], axis=1
    )
    grad_w_k = jnp.concatenate([pick(g_0, item, half, wide) for item in range(2)], axis=1)
    grad_w_v = jnp.concatenate([pick(g_1, item, half, wide) for item in range(2)], axis=1)
    grad_w_o = jnp.concatenate(
        [pick(g, item, wide, wide + half).T for item in range(2) for g in (g_0, g_1)], axis=0
    )
    return (out_rows[None], grad_rows[None], grad_w_q, grad_w_k, grad_w_v, grad_w_o)


def solution(mesh):
    in_specs = (
        P(("dp", "fsdp"), "role", None),
        P(("dp", "fsdp"), "role", None),
        P(("dp", "fsdp"), "role"),
        P(("dp", "fsdp"), "role"),
        P(),
        P(),
        P(),
        P("fsdp", "role"),
        P("fsdp", "role"),
        P("fsdp", "role"),
        P("role", "fsdp"),
    )
    out_specs = (
        P(("dp", "fsdp"), "role", None),
        P(("dp", "fsdp"), "role", None),
        P("fsdp", "role"),
        P("fsdp", "role"),
        P("fsdp", "role"),
        P("role", "fsdp"),
    )
    return jax.shard_map(
        on_device, mesh=mesh, in_specs=in_specs, out_specs=out_specs, check_vma=False
    )
```

```python
from functools import partial

import jax
import jax.numpy as jnp
from jax import lax
from jax.experimental import pallas as pl
from jax.experimental.pallas import tpu as pltpu
from jax.sharding import PartitionSpec as P

HD = 128
TRAJ = 128
NX = 4
NC = 2
NY = 4
NZ = 4

eps_norm = 1e-06
theta_base = 1000000.0
f32 = jnp.float32
bf16 = jnp.bfloat16


def dims(a, b, left, right):
    return lax.dot_general(left, right, (((a,), (b,)), ((), ())), preferred_element_type=f32)


def dot(left, right):
    return dims(1, 0, left, right)


def dot_rows(left, right):
    return dims(1, 1, left, right)


def dot_cols(left, right):
    return dims(0, 0, left, right)


def call(kernel, outs, vmem, scalars=1, macs=0, **more):
    return pl.pallas_call(
        kernel,
        cost_estimate=pl.CostEstimate(
            flops=2 * macs,
            bytes_accessed=sum(shape[0] * shape[1] for shape, _ in outs) * 2,
            transcendentals=0,
        ),
        out_shape=[jax.ShapeDtypeStruct(shape, kind) for shape, kind in outs],
        in_specs=[pl.BlockSpec(memory_space=pltpu.SMEM)] * scalars
        + [pl.BlockSpec()] * (vmem - scalars),
        out_specs=[pl.BlockSpec()] * len(outs),
        compiler_params=pltpu.CompilerParams(vmem_limit_bytes=56 << 20),
        **more,
    )


def turned(place_ref, j):
    row = lax.rem(place_ref[0] + j // NZ, NY)
    col = lax.rem(place_ref[1] + j % NZ, NZ)
    return pl.ds(pl.multiple_of((row * NZ + col) * HD, HD), HD)


def rows_kernel(place_ref, rows_ref, gain_ref, cot_ref, weight_ref, out_ref):
    x = rows_ref[...].astype(f32)
    inv = lax.rsqrt(jnp.mean(x * x, axis=-1, keepdims=True) + eps_norm)
    weight = weight_ref[...]
    for j in range(NY * NZ):
        at = turned(place_ref, j)
        cols = slice(j * HD, (j + 1) * HD)
        out_ref[:TRAJ, cols] = (rows_ref[:, at].astype(f32) * inv * gain_ref[:, at]).astype(bf16)
        out_ref[TRAJ:, cols] = (cot_ref[:, at].astype(f32) * weight).astype(bf16)


def tokens_of(pair_ref, part, cols):
    tops = [(2 * k + part) * TRAJ for k in range(NX)]
    return jnp.concatenate([pair_ref[top : top + TRAJ, cols] for top in tops], axis=0)


def finish_kernel(
    place_ref, rows_ref, gain_ref, cot_ref, weight_ref, total_ref, out_ref, grad_ref, scaled_ref
):
    for j in range(NY * NZ):
        at = turned(place_ref, j)
        cols = slice(j * HD, (j + 1) * HD)
        mixed, back = total_ref[:TRAJ, cols].astype(f32), total_ref[TRAJ:, cols].astype(f32)
        out_ref[:, at] = (rows_ref[:, at].astype(f32) + mixed).astype(bf16)
        scaled_ref[:, at] = back * gain_ref[:, at]
    x = rows_ref[...].astype(f32)
    inv = lax.rsqrt(jnp.mean(x * x, axis=-1, keepdims=True) + eps_norm)
    scaled = scaled_ref[...]
    unit = x * inv
    mean = jnp.mean(scaled * unit, axis=-1, keepdims=True)
    grad_out = (cot_ref[...].astype(f32) * weight_ref[...]).astype(bf16).astype(f32)
    grad_ref[...] = (grad_out + inv * (scaled - unit * mean)).astype(bf16)


def project_kernel(part, pair_ref, *refs):
    own, other, outs = refs[:NY], refs[NY : 2 * NY], refs[2 * NY :]
    totals = [None, None]
    for j in range(NY):
        span = own[j].shape[0]
        left = tokens_of(pair_ref, part, slice(j * span, (j + 1) * span))
        for side, chunks in enumerate((own, other)):
            term = dot(left, chunks[j][...])
            totals[side] = term if totals[side] is None else totals[side] + term
    for out_ref, total in zip(outs, totals):
        out_ref[...] = total.astype(out_ref.dtype)


def expand_kernel(mixed_own_ref, mixed_other_ref, g_own_ref, g_other_ref, *refs):
    out_ref = refs[4 * NY]
    lefts = ((mixed_own_ref, mixed_other_ref), (g_own_ref, g_other_ref))
    for part, (left_own_ref, left_other_ref) in enumerate(lefts):
        own = refs[2 * part * NY : (2 * part + 1) * NY]
        other = refs[(2 * part + 1) * NY : (2 * part + 2) * NY]
        for j in range(NY):
            span = own[j].shape[0]
            total = dot_rows(left_own_ref[...], own[j][...])
            total = total + dot_rows(left_other_ref[...], other[j][...])
            for k in range(NX):
                top = (2 * k + part) * TRAJ
                out_ref[top : top + TRAJ, j * span : (j + 1) * span] = total[
                    k * TRAJ : (k + 1) * TRAJ
                ].astype(bf16)


def rotate(t, cos, sin):
    return t * cos + pltpu.roll(t, HD // 2, 1) * sin


def rotate_back(g, cos, sin):
    return g * cos + pltpu.roll(g * sin, HD // 2, 1)


def inv_norm(t):
    return lax.rsqrt(jnp.mean(t * t, axis=-1, keepdims=True) + eps_norm)


def norm_back(t, grad, gain):
    r = inv_norm(t)
    u = grad * gain
    return r * u - t * (r * r * r * jnp.mean(t * u, axis=-1, keepdims=True))


def stack_heads(own_ref, other_ref):
    return jnp.concatenate(
        [ref[:, k * HD : (k + 1) * HD] for ref in (own_ref, other_ref) for k in range(2)], axis=0
    )


def attend_kernel(
    first_ref, own_ref, other_ref, q_gain_ref, k_gain_ref, cos_ref, sin_ref,
    q_rot_ref, k_rot_ref, value_ref, probs_ref, mixed_own_ref, mixed_other_ref,
):
    cos, sin = cos_ref[...], sin_ref[...]
    cos4, sin4 = jnp.concatenate([cos] * 4, axis=0), jnp.concatenate([sin] * 4, axis=0)
    first = first_ref[0] == 1
    tail_own, tail_other = own_ref[:, 2 * HD :], other_ref[:, 2 * HD :]
    keys = jnp.where(first, tail_own, tail_other)
    value = jnp.where(first, tail_other, tail_own).astype(bf16)
    query = stack_heads(own_ref, other_ref)
    q_rot = rotate(query * inv_norm(query) * q_gain_ref[...], cos4, sin4).astype(bf16)
    k_rot = rotate(keys * inv_norm(keys) * k_gain_ref[...], cos, sin).astype(bf16)
    scores = dot_rows(q_rot, k_rot) * HD ** (-0.5)
    row = lax.broadcasted_iota(jnp.int32, scores.shape, 0) % TRAJ
    allowed = row >= lax.broadcasted_iota(jnp.int32, scores.shape, 1)
    scores = jnp.where(allowed, scores, -1e30)
    peak = jnp.max(scores, axis=-1, keepdims=True)
    weights = jnp.where(allowed, jnp.exp(scores - peak), 0.0)
    probs = weights / jnp.sum(weights, axis=-1, keepdims=True)
    mixed = dot(probs.astype(bf16), value).astype(bf16)
    q_rot_ref[...] = q_rot
    k_rot_ref[...] = k_rot
    value_ref[...] = value
    probs_ref[...] = probs
    for k in range(2):
        mixed_own_ref[:, k * HD : (k + 1) * HD] = mixed[k * TRAJ : (k + 1) * TRAJ]
        mixed_other_ref[:, k * HD : (k + 1) * HD] = mixed[(k + 2) * TRAJ : (k + 3) * TRAJ]


def attend_back_kernel(
    first_ref, own_ref, other_ref, q_gain_ref, k_gain_ref, cos_ref, sin_ref,
    q_rot_ref, k_rot_ref, value_ref, probs_ref, gm_own_ref, gm_other_ref,
    g_own_ref, g_other_ref,
):
    cos, sin = cos_ref[...], sin_ref[...]
    cos4, sin4 = jnp.concatenate([cos] * 4, axis=0), jnp.concatenate([sin] * 4, axis=0)
    first = first_ref[0] == 1
    keys = jnp.where(first, own_ref[:, 2 * HD :], other_ref[:, 2 * HD :])
    query = stack_heads(own_ref, other_ref)
    grad_mixed = stack_heads(gm_own_ref, gm_other_ref)
    q_rot, k_rot, value, probs = q_rot_ref[...], k_rot_ref[...], value_ref[...], probs_ref[...]
    grad_probs = dot_rows(grad_mixed, value)
    grad_value = dot_cols(probs.astype(bf16), grad_mixed).astype(bf16)
    inner = jnp.sum(grad_probs * probs, axis=-1, keepdims=True)
    grad_scores = (probs * (grad_probs - inner) * HD ** (-0.5)).astype(bf16)
    grad_q_rot = dot(grad_scores, k_rot)
    grad_k_rot = dot_cols(grad_scores, q_rot)
    grad_query = norm_back(query, rotate_back(grad_q_rot, cos4, sin4), q_gain_ref[...]).astype(bf16)
    grad_keys = norm_back(keys, rotate_back(grad_k_rot, cos, sin), k_gain_ref[...]).astype(bf16)
    for k in range(2):
        g_own_ref[:, k * HD : (k + 1) * HD] = grad_query[k * TRAJ : (k + 1) * TRAJ]
        g_other_ref[:, k * HD : (k + 1) * HD] = grad_query[(k + 2) * TRAJ : (k + 3) * TRAJ]
    g_own_ref[:, 2 * HD :] = jnp.where(first, grad_keys, grad_value)
    g_other_ref[:, 2 * HD :] = jnp.where(first, grad_value, grad_keys)


def by_trajectory(kernel, outs, ins):
    def spec(rows, cols):
        if rows == 0:
            return pl.BlockSpec(cols, lambda i: (0, 0))
        return pl.BlockSpec((rows, cols), lambda i: (i, 0))

    return pl.pallas_call(
        kernel,
        cost_estimate=pl.CostEstimate(
            flops=2 * 8 * NX * TRAJ * TRAJ * HD * 4, bytes_accessed=1 << 20, transcendentals=0
        ),
        grid=(NX,),
        out_shape=[jax.ShapeDtypeStruct((rows * NX, cols), kind) for rows, cols, kind in outs],
        in_specs=[pl.BlockSpec(memory_space=pltpu.SMEM)] + [spec(*entry) for entry in ins],
        out_specs=[spec(rows, cols) for rows, cols, _ in outs],
        compiler_params=pltpu.CompilerParams(vmem_limit_bytes=56 << 20),
    )


def weight_grad_kernel(pair_ref, own_ref, other_ref, *refs):
    outs, other_out = refs[:NY], refs[NY]
    for j in range(NY):
        span = outs[j].shape[0]
        left = tokens_of(pair_ref, 0, slice(j * span, (j + 1) * span))
        other_out[j * span : (j + 1) * span] = dot_cols(left, other_ref[...]).astype(bf16)
        outs[j][...] = dot_cols(left, own_ref[...]).astype(bf16)


def grad_o_kernel(place_ref, pair_ref, own_ref, other_ref, own_out, other_out):
    span = NZ * HD
    for j in range(NY):
        left = tokens_of(pair_ref, 1, slice(j * span, (j + 1) * span))
        at = pl.ds(pl.multiple_of(lax.rem(place_ref[0] + j, NY) * span, span), span)
        other_out[at] = dot_cols(left, other_ref[...]).astype(bf16)
        own_out[at] = dot_cols(left, own_ref[...]).astype(bf16)


def rope_tables():
    position = jnp.arange(TRAJ, dtype=jnp.int32).astype(f32)
    inverse = jnp.exp(
        jnp.arange(HD // 2, dtype=f32) * (-2.0 * jnp.log(jnp.float32(theta_base)) / HD)
    )
    angles = position[:, None] * inverse[None, :]
    cos, sin = jnp.cos(angles), jnp.sin(angles)
    return jnp.concatenate([cos, cos], axis=1), jnp.concatenate([-sin, sin], axis=1)


def after(values, *earlier):
    alone = not isinstance(values, (list, tuple))
    values = (values,) if alone else tuple(values)
    held = lax.optimization_barrier(values + earlier)[: len(values)]
    return held[0] if alone else list(held)


SAME_CORE = [[x * NC + c for x in range(NX)] for c in range(NC)]


def gather_x(value):
    return lax.all_gather(value, "dp", axis=0, tiled=True, axis_index_groups=SAME_CORE)


SAME_Z = [[y * NZ + z for y in range(NY)] for z in range(NZ)]


def scatter_y(value):
    return lax.psum_scatter(
        value, "fsdp", scatter_dimension=0, tiled=True, axis_index_groups=SAME_Z
    )


def scatter_x(value):
    return lax.psum_scatter(
        value, "dp", scatter_dimension=0, tiled=True, axis_index_groups=SAME_CORE
    )


def take_y(value, step):
    pairs = [(y * NZ + z, (y - step) % NY * NZ + z) for y in range(NY) for z in range(NZ)]
    return lax.ppermute(value, "fsdp", pairs)


def take_z(value, step):
    pairs = [(y * NZ + z, y * NZ + (z - step) % NZ) for y in range(NY) for z in range(NZ)]
    return lax.ppermute(value, "fsdp", pairs)


def other_core(value):
    return lax.ppermute(value, "dp", [(i, i ^ 1) for i in range(NX * NC)])


def owner_role(x):
    return x // (NX // 2)


def from_owner(value):
    n = NX * NC
    pairs = [(owner_role(d // NC) * n + d, (1 - owner_role(d // NC)) * n + d) for d in range(n)]
    return lax.ppermute(value, ("role", "dp"), pairs)


def to_owner(value):
    n = NX * NC
    pairs = [((1 - owner_role(d // NC)) * n + d, owner_role(d // NC) * n + d) for d in range(n)]
    return lax.ppermute(value, ("role", "dp"), pairs)


def spread_x(value, step):
    n = NX * NC
    pairs = [
        (owner_role(x) * n + x * NC + c, owner_role(x) * n + (x - step) % NX * NC + c)
        for x in range(NX)
        for c in range(NC)
    ]
    return lax.ppermute(value, ("role", "dp"), pairs)


def over_role(block, at_owner):
    return jnp.where(at_owner, block, from_owner(block))


def over_z(block):
    return jnp.concatenate([block] + [take_z(block, k) for k in range(1, NZ)], axis=0)


def over_y(plane):
    return [plane] + [take_y(plane, k) for k in range(1, NY)]


def add_core(own, theirs):
    span = own[0].shape[0]
    return [
        (own[k].astype(f32) + theirs[k * span : (k + 1) * span].astype(f32)).astype(bf16)
        for k in range(NY)
    ]


def add_y(terms):
    total = terms[0].astype(f32)
    for term in terms[1:]:
        total = total + term.astype(f32)
    span = total.shape[0] // NZ
    return [total[k * span : (k + 1) * span].astype(bf16) for k in range(NZ)]


def add_z(terms):
    total = terms[0].astype(f32)
    for k in range(1, NZ):
        total = total + take_z(terms[k], -k).astype(f32)
    return total.astype(bf16)


def add_role(term):
    return (term.astype(f32) + to_owner(term).astype(f32)).astype(bf16)


def share(total, x, role, *earlier):
    copies = [total] + after([spread_x(total, k) for k in range(1, NX)], *earlier)
    items = []
    for sub in range(2):
        source = role * 2 + sub
        item = copies[0]
        for k in range(1, NX):
            item = jnp.where((source - x) % NX == k, copies[k], item)
        items.append(item)
    mine = jnp.concatenate(items, axis=0)
    return mine, other_core(mine)


def on_device(rows, cotangent, advantage, action, norm_gain, q_gain, k_gain, w_q, w_k, w_v, w_o):
    role = lax.axis_index("role")
    dp = lax.axis_index("dp")
    fsdp = lax.axis_index("fsdp")
    x, core = dp // NC, dp % NC
    y, z = fsdp // NZ, fsdp % NZ
    at_owner = role == owner_role(x)
    sub = x % 2
    width = 4 * HD
    half = 2 * HD
    first = core == 0
    place = jnp.stack([y, z]).astype(jnp.int32)
    flag = first.astype(jnp.int32)[None]

    q_part = lax.dynamic_slice(w_q, (0, sub * width + core * half), (HD, half))
    k_part = lax.dynamic_slice(w_k, (0, sub * HD), (HD, HD))
    v_part = lax.dynamic_slice(w_v, (0, sub * HD), (HD, HD))
    o_part = lax.dynamic_slice(w_o, (sub * width + core * half, 0), (half, HD)).T
    wide = half + HD
    kv_part = jnp.where(first, k_part, v_part)
    block_part = jnp.concatenate([q_part, kv_part, o_part], axis=1)
    block = over_role(block_part, at_owner)
    qkv_plane = over_z(block[:, :wide])

    rows_own, cot_own = rows[0], cotangent[0]
    gain = norm_gain[None]
    weight = (advantage[0] * action[0].astype(f32))[:, None]
    flat = (TRAJ, rows_own.shape[1])
    pair_own = call(rows_kernel, [((2 * TRAJ, flat[1]), bf16)], 5)(
        place, after(rows_own, block_part), gain, cot_own, weight
    )[0]
    pair = gather_x(pair_own)

    qkv_own = over_y(qkv_plane)
    qkv_first = other_core(qkv_plane)
    o_plane = over_z(after(block[:, wide:], qkv_first))
    o_first = other_core(o_plane)
    qkv_other = [qkv_first] + [other_core(after(piece, o_first)) for piece in qkv_own[1:]]
    o_late = after(o_plane, *qkv_own)
    o_near = [take_y(o_late, 1), take_y(o_late, 3)]

    tokens = pair.shape[0] // 2
    cos_tab, sin_tab = rope_tables()
    proj_own, proj_other = call(
        partial(project_kernel, 0), [((tokens, wide), f32)] * 2, 1 + 2 * NY, scalars=0, macs=tokens * flat[1] * 2 * wide
    )(pair, *qkv_own, *qkv_other)
    o_own = [o_plane, o_near[0], take_y(after(o_plane, proj_own), 2), o_near[1]]
    o_other = [o_first] + [other_core(after(piece, proj_own)) for piece in o_own[1:]]
    proj_own, proj_other = after([proj_own, proj_other], *o_near)
    shared = [(0, (1, HD)), (0, (1, HD)), (0, (TRAJ, HD)), (0, (TRAJ, HD))]
    tables = (q_gain[None], k_gain[None], cos_tab, sin_tab)
    kept = [(width, HD, bf16), (TRAJ, HD, bf16), (TRAJ, HD, bf16), (width, HD, f32)]
    q_rot, k_rot, value, probs, mixed_own, mixed_other = by_trajectory(
        attend_kernel,
        kept + [(TRAJ, half, bf16)] * 2,
        [(TRAJ, wide)] * 2 + shared,
    )(flag, proj_own, proj_other, *tables)

    span = NZ * HD
    go_own, go_cross = call(
        grad_o_kernel, [((NY * span, half), bf16)] * 2, 4, macs=tokens * flat[1] * width
    )(place, after(pair, o_own[2], o_other[1], o_other[3]), mixed_own, mixed_other)
    gm_own, gm_other = call(
        partial(project_kernel, 1), [((tokens, half), bf16)] * 2, 1 + 2 * NY, scalars=0, macs=tokens * flat[1] * width
    )(after(pair, go_cross), *o_own, *o_other)
    go_theirs = after(other_core(go_cross), gm_own)
    go_terms = scatter_y((go_own.astype(f32) + go_theirs.astype(f32)).astype(bf16))
    g_own, g_other = by_trajectory(
        attend_back_kernel,
        [(TRAJ, wide, bf16)] * 2,
        [(TRAJ, wide)] * 2 + shared + [entry[:2] for entry in kept] + [(TRAJ, half)] * 2,
    )(flag, proj_own, proj_other, *tables, q_rot, k_rot, value, probs, *after([gm_own, gm_other], go_theirs))
    *gw_own, gw_cross = call(
        weight_grad_kernel,
        [((span, wide), bf16)] * NY + [((NY * span, wide), bf16)],
        3,
        scalars=0,
    )(pair, g_own, g_other)
    gw_theirs = other_core(gw_cross)
    terms = call(
        expand_kernel,
        [((2 * tokens, flat[1]), bf16)],
        4 + 4 * NY,
        scalars=0,
        macs=tokens * flat[1] * (width + 2 * wide),
    )(mixed_own, mixed_other, *after([g_own, g_other], gw_cross), *o_own, *o_other, *qkv_own, *qkv_other)[0]
    row_total = scatter_x(terms)

    gw_terms = after(add_core(gw_own, gw_theirs), terms)
    gw_near = [take_y(gw_terms[1], -1), take_y(gw_terms[3], -3)]
    go_terms = after(go_terms, *gw_near)
    go_term = add_z([go_terms[k * HD : (k + 1) * HD] for k in range(NZ)])
    gw_far = take_y(after(gw_terms[2], *gw_near), -2)
    gw_terms = add_y([gw_terms[0], *gw_near, after(gw_far, go_term)])
    gw_term = add_z(gw_terms)
    out_rows, grad_rows = call(
        finish_kernel, [(flat, bf16)] * 2, 6, scratch_shapes=[pltpu.VMEM(flat, f32)]
    )(place, rows_own, gain, cot_own, weight, row_total)
    total = add_role(jnp.concatenate([gw_term, go_term], axis=1))
    mine, theirs = share(total, x, role, grad_rows)
    g_0, g_1 = jnp.where(first, mine, theirs), jnp.where(first, theirs, mine)

    def pick(value, item, lo, hi):
        return value[item * HD : (item + 1) * HD, lo:hi].astype(f32)

    grad_w_q = jnp.concatenate(
        [pick(g, item, 0, half) for item in range(2) for g in (g_0, g_1)], axis=1
    )
    grad_w_k = jnp.concatenate([pick(g_0, item, half, wide) for item in range(2)], axis=1)
    grad_w_v = jnp.concatenate([pick(g_1, item, half, wide) for item in range(2)], axis=1)
    grad_w_o = jnp.concatenate(
        [pick(g, item, wide, wide + half).T for item in range(2) for g in (g_0, g_1)], axis=0
    )
    return (out_rows[None], grad_rows[None], grad_w_q, grad_w_k, grad_w_v, grad_w_o)


def solution(mesh):
    in_specs = (
        P(("dp", "fsdp"), "role", None),
        P(("dp", "fsdp"), "role", None),
        P(("dp", "fsdp"), "role"),
        P(("dp", "fsdp"), "role"),
        P(),
        P(),
        P(),
        P("fsdp", "role"),
        P("fsdp", "role"),
        P("fsdp", "role"),
        P("role", "fsdp"),
    )
    out_specs = (
        P(("dp", "fsdp"), "role", None),
        P(("dp", "fsdp"), "role", None),
        P("fsdp", "role"),
        P("fsdp", "role"),
        P("fsdp", "role"),
        P("role", "fsdp"),
    )
    return jax.shard_map(
        on_device, mesh=mesh, in_specs=in_specs, out_specs=out_specs, check_vma=False
    )
```

```python
import jax
import jax.numpy as jnp
from jax import lax
from jax.experimental import pallas as pl
from jax.experimental.pallas import tpu as pltpu
from jax.sharding import PartitionSpec as P

HD = 128
TRAJ = 128
NX = 4
NC = 2
NY = 4
NZ = 4

eps_norm = 1e-06
theta_base = 1000000.0
f32 = jnp.float32
bf16 = jnp.bfloat16


def dims(a, b, left, right):
    return lax.dot_general(left, right, (((a,), (b,)), ((), ())), preferred_element_type=f32)


def dot(left, right):
    return dims(1, 0, left, right)


def dot_rows(left, right):
    return dims(1, 1, left, right)


def dot_cols(left, right):
    return dims(0, 0, left, right)


def call(kernel, outs, vmem, scalars=1, macs=0, parts=(), **more):
    return pl.pallas_call(
        kernel,
        grid=(1,) if parts else (),
        cost_estimate=pl.CostEstimate(
            flops=2 * macs,
            bytes_accessed=sum(shape[0] * shape[1] for shape, _ in outs) * 2,
            transcendentals=0,
        ),
        out_shape=[jax.ShapeDtypeStruct(shape, kind) for shape, kind in outs],
        in_specs=[pl.BlockSpec(memory_space=pltpu.SMEM)] * scalars
        + [part_spec(*entry) for entry in parts]
        + [pl.BlockSpec()] * (vmem - scalars - len(parts)),
        out_specs=[pl.BlockSpec()] * len(outs),
        compiler_params=pltpu.CompilerParams(vmem_limit_bytes=56 << 20),
        **more,
    )


def turned(place_ref, j):
    row = lax.rem(place_ref[0] + j // NZ, NY)
    col = lax.rem(place_ref[1] + j % NZ, NZ)
    return pl.ds(pl.multiple_of((row * NZ + col) * HD, HD), HD)


def rows_kernel(place_ref, rows_ref, gain_ref, cot_ref, weight_ref, out_ref):
    x = rows_ref[...].astype(f32)
    inv = lax.rsqrt(jnp.mean(x * x, axis=-1, keepdims=True) + eps_norm)
    weight = weight_ref[...]
    for j in range(NY * NZ):
        at = turned(place_ref, j)
        cols = slice(j * HD, (j + 1) * HD)
        out_ref[:TRAJ, cols] = (rows_ref[:, at].astype(f32) * inv * gain_ref[:, at]).astype(bf16)
        out_ref[TRAJ:, cols] = (cot_ref[:, at].astype(f32) * weight).astype(bf16)


def part_spec(part, columns):
    return pl.BlockSpec((NX, 1, TRAJ, columns), lambda i: (0, part, 0, 0))


def tokens_of(part_ref, cols):
    return jnp.concatenate([part_ref[k, 0, :, cols] for k in range(NX)], axis=0)


def finish_kernel(
    place_ref, rows_ref, gain_ref, cot_ref, weight_ref, total_ref, out_ref, grad_ref, scaled_ref
):
    for j in range(NY * NZ):
        at = turned(place_ref, j)
        cols = slice(j * HD, (j + 1) * HD)
        mixed, back = total_ref[:TRAJ, cols].astype(f32), total_ref[TRAJ:, cols].astype(f32)
        out_ref[:, at] = (rows_ref[:, at].astype(f32) + mixed).astype(bf16)
        scaled_ref[:, at] = back * gain_ref[:, at]
    x = rows_ref[...].astype(f32)
    inv = lax.rsqrt(jnp.mean(x * x, axis=-1, keepdims=True) + eps_norm)
    scaled = scaled_ref[...]
    unit = x * inv
    mean = jnp.mean(scaled * unit, axis=-1, keepdims=True)
    grad_out = (cot_ref[...].astype(f32) * weight_ref[...]).astype(bf16).astype(f32)
    grad_ref[...] = (grad_out + inv * (scaled - unit * mean)).astype(bf16)


def project_kernel(part_ref, *refs):
    own, other, outs = refs[:NY], refs[NY : 2 * NY], refs[2 * NY :]
    totals = [None, None]
    for j in range(NY):
        span = own[j].shape[0]
        left = tokens_of(part_ref, slice(j * span, (j + 1) * span))
        for side, chunks in enumerate((own, other)):
            term = dot(left, chunks[j][...])
            totals[side] = term if totals[side] is None else totals[side] + term
    for out_ref, total in zip(outs, totals):
        out_ref[...] = total.astype(out_ref.dtype)


def expand_kernel(mixed_own_ref, mixed_other_ref, g_own_ref, g_other_ref, *refs):
    out_ref = refs[4 * NY]
    lefts = ((mixed_own_ref, mixed_other_ref), (g_own_ref, g_other_ref))
    for part, (left_own_ref, left_other_ref) in enumerate(lefts):
        own = refs[2 * part * NY : (2 * part + 1) * NY]
        other = refs[(2 * part + 1) * NY : (2 * part + 2) * NY]
        for j in range(NY):
            span = own[j].shape[0]
            total = dot_rows(left_own_ref[...], own[j][...])
            total = total + dot_rows(left_other_ref[...], other[j][...])
            for k in range(NX):
                top = (2 * k + part) * TRAJ
                out_ref[top : top + TRAJ, j * span : (j + 1) * span] = total[
                    k * TRAJ : (k + 1) * TRAJ
                ].astype(bf16)


def rotate(t, cos, sin):
    return t * cos + pltpu.roll(t, HD // 2, 1) * sin


def rotate_back(g, cos, sin):
    return g * cos + pltpu.roll(g * sin, HD // 2, 1)


def inv_norm(t):
    return lax.rsqrt(jnp.mean(t * t, axis=-1, keepdims=True) + eps_norm)


def norm_back(t, grad, gain):
    r = inv_norm(t)
    u = grad * gain
    return r * u - t * (r * r * r * jnp.mean(t * u, axis=-1, keepdims=True))


def stack_heads(own_ref, other_ref, rows=slice(None)):
    return jnp.concatenate(
        [ref[rows, k * HD : (k + 1) * HD] for ref in (own_ref, other_ref) for k in range(2)], axis=0
    )


def attend_kernel(
    first_ref, own_ref, other_ref, q_gain_ref, k_gain_ref, cos_ref, sin_ref,
    q_rot_ref, k_rot_ref, value_ref, probs_ref, mixed_own_ref, mixed_other_ref,
):
    cos, sin = cos_ref[...], sin_ref[...]
    cos4, sin4 = jnp.concatenate([cos] * 4, axis=0), jnp.concatenate([sin] * 4, axis=0)
    first = first_ref[0] == 1
    tail_own, tail_other = own_ref[:, 2 * HD :], other_ref[:, 2 * HD :]
    keys = jnp.where(first, tail_own, tail_other)
    value = jnp.where(first, tail_other, tail_own).astype(bf16)
    query = stack_heads(own_ref, other_ref)
    q_rot = rotate(query * inv_norm(query) * q_gain_ref[...], cos4, sin4).astype(bf16)
    k_rot = rotate(keys * inv_norm(keys) * k_gain_ref[...], cos, sin).astype(bf16)
    scores = dot_rows(q_rot, k_rot) * HD ** (-0.5)
    row = lax.broadcasted_iota(jnp.int32, scores.shape, 0) % TRAJ
    allowed = row >= lax.broadcasted_iota(jnp.int32, scores.shape, 1)
    scores = jnp.where(allowed, scores, -1e30)
    peak = jnp.max(scores, axis=-1, keepdims=True)
    weights = jnp.where(allowed, jnp.exp(scores - peak), 0.0)
    probs = weights / jnp.sum(weights, axis=-1, keepdims=True)
    mixed = dot(probs.astype(bf16), value).astype(bf16)
    q_rot_ref[...] = q_rot
    k_rot_ref[...] = k_rot
    value_ref[...] = value
    probs_ref[...] = probs
    for k in range(2):
        mixed_own_ref[:, k * HD : (k + 1) * HD] = mixed[k * TRAJ : (k + 1) * TRAJ]
        mixed_other_ref[:, k * HD : (k + 1) * HD] = mixed[(k + 2) * TRAJ : (k + 3) * TRAJ]


def back_kernel(
    first_ref, normed_ref, grad_ref, own_ref, other_ref, q_gain_ref, k_gain_ref, cos_ref, sin_ref,
    q_rot_ref, k_rot_ref, value_ref, probs_ref, *refs,
):
    o_own, o_other, refs = refs[:NY], refs[NY : 2 * NY], refs[2 * NY :]
    g_own_ref, g_other_ref, outs, other_out = refs[0], refs[1], refs[2 : 2 + NY], refs[2 + NY]
    gm_own_ref, gm_other_ref = refs[3 + NY :]
    project_kernel(grad_ref, *o_own, *o_other, gm_own_ref, gm_other_ref)
    cos, sin = cos_ref[...], sin_ref[...]
    cos4, sin4 = jnp.concatenate([cos] * 4, axis=0), jnp.concatenate([sin] * 4, axis=0)
    first = first_ref[0] == 1
    for i in range(NX):
        at = slice(i * TRAJ, (i + 1) * TRAJ)
        at4 = slice(i * 4 * TRAJ, (i + 1) * 4 * TRAJ)
        keys = jnp.where(first, own_ref[at, 2 * HD :], other_ref[at, 2 * HD :])
        query = stack_heads(own_ref, other_ref, at)
        grad_mixed = stack_heads(gm_own_ref, gm_other_ref, at)
        q_rot, k_rot, value, probs = q_rot_ref[at4], k_rot_ref[at], value_ref[at], probs_ref[at4]
        grad_probs = dot_rows(grad_mixed, value)
        grad_value = dot_cols(probs.astype(bf16), grad_mixed).astype(bf16)
        inner = jnp.sum(grad_probs * probs, axis=-1, keepdims=True)
        grad_scores = (probs * (grad_probs - inner) * HD ** (-0.5)).astype(bf16)
        grad_q_rot = rotate_back(dot(grad_scores, k_rot), cos4, sin4)
        grad_k_rot = rotate_back(dot_cols(grad_scores, q_rot), cos, sin)
        grad_query = norm_back(query, grad_q_rot, q_gain_ref[...]).astype(bf16)
        grad_keys = norm_back(keys, grad_k_rot, k_gain_ref[...]).astype(bf16)
        for k in range(2):
            g_own_ref[at, k * HD : (k + 1) * HD] = grad_query[k * TRAJ : (k + 1) * TRAJ]
            g_other_ref[at, k * HD : (k + 1) * HD] = grad_query[(k + 2) * TRAJ : (k + 3) * TRAJ]
        g_own_ref[at, 2 * HD :] = jnp.where(first, grad_keys, grad_value)
        g_other_ref[at, 2 * HD :] = jnp.where(first, grad_value, grad_keys)
    for j in range(NY):
        span = outs[j].shape[0]
        left = tokens_of(normed_ref, slice(j * span, (j + 1) * span))
        other_out[j * span : (j + 1) * span] = dot_cols(left, g_other_ref[...]).astype(bf16)
        outs[j][...] = dot_cols(left, g_own_ref[...]).astype(bf16)


def by_trajectory(kernel, outs, ins):
    def spec(rows, cols):
        if rows == 0:
            return pl.BlockSpec(cols, lambda i: (0, 0))
        return pl.BlockSpec((rows, cols), lambda i: (i, 0))

    return pl.pallas_call(
        kernel,
        cost_estimate=pl.CostEstimate(
            flops=2 * 8 * NX * TRAJ * TRAJ * HD * 4, bytes_accessed=1 << 20, transcendentals=0
        ),
        grid=(NX,),
        out_shape=[jax.ShapeDtypeStruct((rows * NX, cols), kind) for rows, cols, kind in outs],
        in_specs=[pl.BlockSpec(memory_space=pltpu.SMEM)] + [spec(*entry) for entry in ins],
        out_specs=[spec(rows, cols) for rows, cols, _ in outs],
        compiler_params=pltpu.CompilerParams(vmem_limit_bytes=56 << 20),
    )


def grad_o_kernel(place_ref, part_ref, own_ref, other_ref, own_out, other_out):
    span = NZ * HD
    for j in range(NY):
        left = tokens_of(part_ref, slice(j * span, (j + 1) * span))
        at = pl.ds(pl.multiple_of(lax.rem(place_ref[0] + j, NY) * span, span), span)
        other_out[at] = dot_cols(left, other_ref[...]).astype(bf16)
        own_out[at] = dot_cols(left, own_ref[...]).astype(bf16)


def rope_tables():
    position = jnp.arange(TRAJ, dtype=jnp.int32).astype(f32)
    inverse = jnp.exp(
        jnp.arange(HD // 2, dtype=f32) * (-2.0 * jnp.log(jnp.float32(theta_base)) / HD)
    )
    angles = position[:, None] * inverse[None, :]
    cos, sin = jnp.cos(angles), jnp.sin(angles)
    return jnp.concatenate([cos, cos], axis=1), jnp.concatenate([-sin, sin], axis=1)


def after(values, *earlier):
    alone = not isinstance(values, (list, tuple))
    values = (values,) if alone else tuple(values)
    held = lax.optimization_barrier(values + earlier)[: len(values)]
    return held[0] if alone else list(held)


SAME_CORE = [[x * NC + c for x in range(NX)] for c in range(NC)]


def gather_x(value):
    return lax.all_gather(value, "dp", axis=0, tiled=True, axis_index_groups=SAME_CORE)


SAME_Z = [[y * NZ + z for y in range(NY)] for z in range(NZ)]


def scatter_y(value):
    return lax.psum_scatter(
        value, "fsdp", scatter_dimension=0, tiled=True, axis_index_groups=SAME_Z
    )


def scatter_x(value):
    return lax.psum_scatter(
        value, "dp", scatter_dimension=0, tiled=True, axis_index_groups=SAME_CORE
    )


def take_y(value, step):
    pairs = [(y * NZ + z, (y - step) % NY * NZ + z) for y in range(NY) for z in range(NZ)]
    return lax.ppermute(value, "fsdp", pairs)


def take_z(value, step):
    pairs = [(y * NZ + z, y * NZ + (z - step) % NZ) for y in range(NY) for z in range(NZ)]
    return lax.ppermute(value, "fsdp", pairs)


def other_core(value):
    return lax.ppermute(value, "dp", [(i, i ^ 1) for i in range(NX * NC)])


def owner_role(x):
    return x // (NX // 2)


def from_owner(value):
    n = NX * NC
    pairs = [(owner_role(d // NC) * n + d, (1 - owner_role(d // NC)) * n + d) for d in range(n)]
    return lax.ppermute(value, ("role", "dp"), pairs)


def to_owner(value):
    n = NX * NC
    pairs = [((1 - owner_role(d // NC)) * n + d, owner_role(d // NC) * n + d) for d in range(n)]
    return lax.ppermute(value, ("role", "dp"), pairs)


def spread_x(value, step):
    n = NX * NC
    pairs = [
        (owner_role(x) * n + x * NC + c, owner_role(x) * n + (x - step) % NX * NC + c)
        for x in range(NX)
        for c in range(NC)
    ]
    return lax.ppermute(value, ("role", "dp"), pairs)


def over_role(block, at_owner):
    return jnp.where(at_owner, block, from_owner(block))


def over_z(block):
    return jnp.concatenate([block] + [take_z(block, k) for k in range(1, NZ)], axis=0)


def over_y(plane):
    return [plane] + [take_y(plane, k) for k in range(1, NY)]


def add_core(own, theirs):
    span = own[0].shape[0]
    return [
        (own[k].astype(f32) + theirs[k * span : (k + 1) * span].astype(f32)).astype(bf16)
        for k in range(NY)
    ]


def add_y(terms):
    total = terms[0].astype(f32)
    for term in terms[1:]:
        total = total + term.astype(f32)
    span = total.shape[0] // NZ
    return [total[k * span : (k + 1) * span].astype(bf16) for k in range(NZ)]


def add_z(terms):
    total = terms[0].astype(f32)
    for k in range(1, NZ):
        total = total + take_z(terms[k], -k).astype(f32)
    return total.astype(bf16)


def add_role(term):
    return (term.astype(f32) + to_owner(term).astype(f32)).astype(bf16)


def share(total, x, role, *earlier):
    copies = [total] + after([spread_x(total, k) for k in range(1, NX)], *earlier)
    items = []
    for sub in range(2):
        source = role * 2 + sub
        item = copies[0]
        for k in range(1, NX):
            item = jnp.where((source - x) % NX == k, copies[k], item)
        items.append(item)
    mine = jnp.concatenate(items, axis=0)
    return mine, other_core(mine)


def on_device(rows, cotangent, advantage, action, norm_gain, q_gain, k_gain, w_q, w_k, w_v, w_o):
    role = lax.axis_index("role")
    dp = lax.axis_index("dp")
    fsdp = lax.axis_index("fsdp")
    x, core = dp // NC, dp % NC
    y, z = fsdp // NZ, fsdp % NZ
    at_owner = role == owner_role(x)
    sub = x % 2
    width = 4 * HD
    half = 2 * HD
    first = core == 0
    place = jnp.stack([y, z]).astype(jnp.int32)
    flag = first.astype(jnp.int32)[None]

    q_part = lax.dynamic_slice(w_q, (0, sub * width + core * half), (HD, half))
    k_part = lax.dynamic_slice(w_k, (0, sub * HD), (HD, HD))
    v_part = lax.dynamic_slice(w_v, (0, sub * HD), (HD, HD))
    o_part = lax.dynamic_slice(w_o, (sub * width + core * half, 0), (half, HD)).T
    wide = half + HD
    kv_part = jnp.where(first, k_part, v_part)
    block_part = jnp.concatenate([q_part, kv_part, o_part], axis=1)
    block = over_role(block_part, at_owner)
    qkv_plane = over_z(block[:, :wide])

    rows_own, cot_own = rows[0], cotangent[0]
    gain = norm_gain[None]
    weight = (advantage[0] * action[0].astype(f32))[:, None]
    flat = (TRAJ, rows_own.shape[1])
    pair_own = call(rows_kernel, [((2 * TRAJ, flat[1]), bf16)], 5)(
        place, after(rows_own, block_part), gain, cot_own, weight
    )[0]
    pair = gather_x(pair_own)

    qkv_own = over_y(qkv_plane)
    qkv_first = other_core(qkv_plane)
    o_plane = over_z(after(block[:, wide:], qkv_first))
    o_first = other_core(o_plane)
    qkv_other = [qkv_first] + [other_core(after(piece, o_first)) for piece in qkv_own[1:]]
    o_late = after(o_plane, *qkv_own)
    o_near = [take_y(o_late, 1), take_y(o_late, 3)]

    tokens = pair.shape[0] // 2
    pair = pair.reshape(NX, 2, TRAJ, flat[1])
    cos_tab, sin_tab = rope_tables()
    proj_own, proj_other = call(
        project_kernel,
        [((tokens, wide), f32)] * 2,
        1 + 2 * NY,
        scalars=0,
        macs=tokens * flat[1] * 2 * wide,
        parts=[(0, flat[1])],
    )(pair, *qkv_own, *qkv_other)
    o_own = [o_plane, o_near[0], take_y(after(o_plane, proj_own), 2), o_near[1]]
    o_other = [o_first] + [other_core(after(piece, proj_own)) for piece in o_own[1:]]
    proj_own, proj_other = after([proj_own, proj_other], *o_near)
    shared = [(0, (1, HD)), (0, (1, HD)), (0, (TRAJ, HD)), (0, (TRAJ, HD))]
    tables = (q_gain[None], k_gain[None], cos_tab, sin_tab)
    kept = [(width, HD, bf16), (TRAJ, HD, bf16), (TRAJ, HD, bf16), (width, HD, f32)]
    q_rot, k_rot, value, probs, mixed_own, mixed_other = by_trajectory(
        attend_kernel,
        kept + [(TRAJ, half, bf16)] * 2,
        [(TRAJ, wide)] * 2 + shared,
    )(flag, proj_own, proj_other, *tables)

    span = NZ * HD
    go_own, go_cross = call(
        grad_o_kernel,
        [((NY * span, half), bf16)] * 2,
        4,
        macs=tokens * flat[1] * width,
        parts=[(1, flat[1])],
    )(place, after(pair, o_own[2], o_other[1], o_other[3]), mixed_own, mixed_other)
    go_theirs = after(other_core(go_cross), o_other[2])
    go_terms = scatter_y((go_own.astype(f32) + go_theirs.astype(f32)).astype(bf16))
    g_own, g_other, *gw_own, gw_cross = call(
        back_kernel,
        [((tokens, wide), bf16)] * 2
        + [((span, wide), bf16)] * NY
        + [((NY * span, wide), bf16)],
        13 + 2 * NY,
        macs=tokens * flat[1] * (width + 2 * wide),
        parts=[(0, flat[1]), (1, flat[1])],
        scratch_shapes=[pltpu.VMEM((tokens, half), bf16)] * 2,
    )(
        flag,
        *after([pair, pair], go_theirs),
        proj_own,
        proj_other,
        *tables,
        q_rot,
        k_rot,
        value,
        probs,
        *o_own,
        *o_other,
    )
    gw_theirs = other_core(gw_cross)
    terms = call(
        expand_kernel,
        [((2 * tokens, flat[1]), bf16)],
        4 + 4 * NY,
        scalars=0,
        macs=tokens * flat[1] * (width + 2 * wide),
    )(mixed_own, mixed_other, *after([g_own, g_other], gw_cross), *o_own, *o_other, *qkv_own, *qkv_other)[0]
    row_total = scatter_x(terms)

    gw_terms = after(add_core(gw_own, gw_theirs), terms)
    gw_near = [take_y(gw_terms[1], -1), take_y(gw_terms[3], -3)]
    go_terms = after(go_terms, *gw_near)
    go_term = add_z([go_terms[k * HD : (k + 1) * HD] for k in range(NZ)])
    gw_far = take_y(after(gw_terms[2], *gw_near), -2)
    gw_terms = add_y([gw_terms[0], *gw_near, after(gw_far, go_term)])
    gw_term = add_z(gw_terms)
    out_rows, grad_rows = call(
        finish_kernel, [(flat, bf16)] * 2, 6, scratch_shapes=[pltpu.VMEM(flat, f32)]
    )(place, rows_own, gain, cot_own, weight, row_total)
    total = add_role(jnp.concatenate([gw_term, go_term], axis=1))
    mine, theirs = share(total, x, role, grad_rows)
    g_0, g_1 = jnp.where(first, mine, theirs), jnp.where(first, theirs, mine)

    def pick(value, item, lo, hi):
        return value[item * HD : (item + 1) * HD, lo:hi].astype(f32)

    grad_w_q = jnp.concatenate(
        [pick(g, item, 0, half) for item in range(2) for g in (g_0, g_1)], axis=1
    )
    grad_w_k = jnp.concatenate([pick(g_0, item, half, wide) for item in range(2)], axis=1)
    grad_w_v = jnp.concatenate([pick(g_1, item, half, wide) for item in range(2)], axis=1)
    grad_w_o = jnp.concatenate(
        [pick(g, item, wide, wide + half).T for item in range(2) for g in (g_0, g_1)], axis=0
    )
    return (out_rows[None], grad_rows[None], grad_w_q, grad_w_k, grad_w_v, grad_w_o)


def solution(mesh):
    in_specs = (
        P(("dp", "fsdp"), "role", None),
        P(("dp", "fsdp"), "role", None),
        P(("dp", "fsdp"), "role"),
        P(("dp", "fsdp"), "role"),
        P(),
        P(),
        P(),
        P("fsdp", "role"),
        P("fsdp", "role"),
        P("fsdp", "role"),
        P("role", "fsdp"),
    )
    out_specs = (
        P(("dp", "fsdp"), "role", None),
        P(("dp", "fsdp"), "role", None),
        P("fsdp", "role"),
        P("fsdp", "role"),
        P("fsdp", "role"),
        P("role", "fsdp"),
    )
    return jax.shard_map(
        on_device, mesh=mesh, in_specs=in_specs, out_specs=out_specs, check_vma=False
    )
```

```python
import jax
import jax.numpy as jnp
from jax import lax
from jax.experimental import pallas as pl
from jax.experimental.pallas import tpu as pltpu
from jax.sharding import PartitionSpec as P

HD = 128
TRAJ = 128
NX = 4
NC = 2
NY = 4
NZ = 4

eps_norm = 1e-06
theta_base = 1000000.0
f32 = jnp.float32
bf16 = jnp.bfloat16


def dims(a, b, left, right):
    return lax.dot_general(left, right, (((a,), (b,)), ((), ())), preferred_element_type=f32)


def dot(left, right):
    return dims(1, 0, left, right)


def dot_rows(left, right):
    return dims(1, 1, left, right)


def dot_cols(left, right):
    return dims(0, 0, left, right)


def call(kernel, outs, vmem, scalars=1, macs=0, parts=(), **more):
    return pl.pallas_call(
        kernel,
        grid=(1,) if parts else (),
        cost_estimate=pl.CostEstimate(
            flops=2 * macs,
            bytes_accessed=sum(shape[0] * shape[1] for shape, _ in outs) * 2,
            transcendentals=0,
        ),
        out_shape=[jax.ShapeDtypeStruct(shape, kind) for shape, kind in outs],
        in_specs=[pl.BlockSpec(memory_space=pltpu.SMEM)] * scalars
        + [part_spec(*entry) for entry in parts]
        + [pl.BlockSpec()] * (vmem - scalars - len(parts)),
        out_specs=[pl.BlockSpec()] * len(outs),
        compiler_params=pltpu.CompilerParams(vmem_limit_bytes=56 << 20),
        **more,
    )


def turned(place_ref, j):
    row = lax.rem(place_ref[0] + j // NZ, NY)
    col = lax.rem(place_ref[1] + j % NZ, NZ)
    return pl.ds(pl.multiple_of((row * NZ + col) * HD, HD), HD)


def rows_kernel(place_ref, rows_ref, gain_ref, cot_ref, weight_ref, out_ref):
    x = rows_ref[...].astype(f32)
    inv = lax.rsqrt(jnp.mean(x * x, axis=-1, keepdims=True) + eps_norm)
    weight = weight_ref[...]
    for j in range(NY * NZ):
        at = turned(place_ref, j)
        cols = slice(j * HD, (j + 1) * HD)
        out_ref[:TRAJ, cols] = (rows_ref[:, at].astype(f32) * inv * gain_ref[:, at]).astype(bf16)
        out_ref[TRAJ:, cols] = (cot_ref[:, at].astype(f32) * weight).astype(bf16)


def part_spec(part, columns):
    return pl.BlockSpec((NX, 1, TRAJ, columns), lambda i: (0, part, 0, 0))


def tokens_of(part_ref, cols):
    return jnp.concatenate([part_ref[k, 0, :, cols] for k in range(NX)], axis=0)


def finish_kernel(
    place_ref, rows_ref, gain_ref, cot_ref, weight_ref, total_ref, out_ref, grad_ref, scaled_ref
):
    for j in range(NY * NZ):
        at = turned(place_ref, j)
        cols = slice(j * HD, (j + 1) * HD)
        mixed, back = total_ref[:TRAJ, cols].astype(f32), total_ref[TRAJ:, cols].astype(f32)
        out_ref[:, at] = (rows_ref[:, at].astype(f32) + mixed).astype(bf16)
        scaled_ref[:, at] = back * gain_ref[:, at]
    x = rows_ref[...].astype(f32)
    inv = lax.rsqrt(jnp.mean(x * x, axis=-1, keepdims=True) + eps_norm)
    scaled = scaled_ref[...]
    unit = x * inv
    mean = jnp.mean(scaled * unit, axis=-1, keepdims=True)
    grad_out = (cot_ref[...].astype(f32) * weight_ref[...]).astype(bf16).astype(f32)
    grad_ref[...] = (grad_out + inv * (scaled - unit * mean)).astype(bf16)


def project_kernel(part_ref, *refs):
    own, other, outs = refs[:NY], refs[NY : 2 * NY], refs[2 * NY :]
    totals = [None, None]
    for j in range(NY):
        span = own[j].shape[0]
        left = tokens_of(part_ref, slice(j * span, (j + 1) * span))
        for side, chunks in enumerate((own, other)):
            term = dot(left, chunks[j][...])
            totals[side] = term if totals[side] is None else totals[side] + term
    for out_ref, total in zip(outs, totals):
        out_ref[...] = total.astype(out_ref.dtype)


def expand_kernel(mixed_own_ref, mixed_other_ref, g_own_ref, g_other_ref, *refs):
    out_ref = refs[4 * NY]
    lefts = ((mixed_own_ref, mixed_other_ref), (g_own_ref, g_other_ref))
    for part, (left_own_ref, left_other_ref) in enumerate(lefts):
        own = refs[2 * part * NY : (2 * part + 1) * NY]
        other = refs[(2 * part + 1) * NY : (2 * part + 2) * NY]
        for j in range(NY):
            span = own[j].shape[0]
            total = dot_rows(left_own_ref[...], own[j][...])
            total = total + dot_rows(left_other_ref[...], other[j][...])
            for k in range(NX):
                top = (2 * k + part) * TRAJ
                out_ref[top : top + TRAJ, j * span : (j + 1) * span] = total[
                    k * TRAJ : (k + 1) * TRAJ
                ].astype(bf16)


def rotate(t, cos, sin):
    return t * cos + pltpu.roll(t, HD // 2, 1) * sin


def rotate_back(g, cos, sin):
    return g * cos + pltpu.roll(g * sin, HD // 2, 1)


def inv_norm(t):
    return lax.rsqrt(jnp.mean(t * t, axis=-1, keepdims=True) + eps_norm)


def norm_back(t, grad, gain):
    r = inv_norm(t)
    u = grad * gain
    return r * u - t * (r * r * r * jnp.mean(t * u, axis=-1, keepdims=True))


def stack_heads(own_ref, other_ref, rows=slice(None)):
    return jnp.concatenate(
        [ref[rows, k * HD : (k + 1) * HD] for ref in (own_ref, other_ref) for k in range(2)], axis=0
    )


def attend_kernel(
    first_ref, own_ref, other_ref, q_gain_ref, k_gain_ref, cos_ref, sin_ref,
    q_rot_ref, k_rot_ref, value_ref, probs_ref, mixed_own_ref, mixed_other_ref,
):
    cos, sin = cos_ref[...], sin_ref[...]
    cos4, sin4 = jnp.concatenate([cos] * 4, axis=0), jnp.concatenate([sin] * 4, axis=0)
    first = first_ref[0] == 1
    tail_own, tail_other = own_ref[:, 2 * HD :], other_ref[:, 2 * HD :]
    keys = jnp.where(first, tail_own, tail_other)
    value = jnp.where(first, tail_other, tail_own).astype(bf16)
    query = stack_heads(own_ref, other_ref)
    q_rot = rotate(query * inv_norm(query) * q_gain_ref[...], cos4, sin4).astype(bf16)
    k_rot = rotate(keys * inv_norm(keys) * k_gain_ref[...], cos, sin).astype(bf16)
    scores = dot_rows(q_rot, k_rot) * HD ** (-0.5)
    row = lax.broadcasted_iota(jnp.int32, scores.shape, 0) % TRAJ
    allowed = row >= lax.broadcasted_iota(jnp.int32, scores.shape, 1)
    scores = jnp.where(allowed, scores, -1e30)
    peak = jnp.max(scores, axis=-1, keepdims=True)
    weights = jnp.where(allowed, jnp.exp(scores - peak), 0.0)
    probs = weights / jnp.sum(weights, axis=-1, keepdims=True)
    mixed = dot(probs.astype(bf16), value).astype(bf16)
    q_rot_ref[...] = q_rot
    k_rot_ref[...] = k_rot
    value_ref[...] = value
    probs_ref[...] = probs
    for k in range(2):
        mixed_own_ref[:, k * HD : (k + 1) * HD] = mixed[k * TRAJ : (k + 1) * TRAJ]
        mixed_other_ref[:, k * HD : (k + 1) * HD] = mixed[(k + 2) * TRAJ : (k + 3) * TRAJ]


def back_kernel(
    first_ref, normed_ref, grad_ref, own_ref, other_ref, q_gain_ref, k_gain_ref, cos_ref, sin_ref,
    q_rot_ref, k_rot_ref, value_ref, probs_ref, *refs,
):
    o_own, o_other, refs = refs[:NY], refs[NY : 2 * NY], refs[2 * NY :]
    g_own_ref, g_other_ref, outs, other_out = refs[0], refs[1], refs[2 : 2 + NY], refs[2 + NY]
    gm_own_ref, gm_other_ref = refs[3 + NY :]
    project_kernel(grad_ref, *o_own, *o_other, gm_own_ref, gm_other_ref)
    cos, sin = cos_ref[...], sin_ref[...]
    cos4, sin4 = jnp.concatenate([cos] * 4, axis=0), jnp.concatenate([sin] * 4, axis=0)
    first = first_ref[0] == 1
    for i in range(NX):
        at = slice(i * TRAJ, (i + 1) * TRAJ)
        at4 = slice(i * 4 * TRAJ, (i + 1) * 4 * TRAJ)
        keys = jnp.where(first, own_ref[at, 2 * HD :], other_ref[at, 2 * HD :])
        query = stack_heads(own_ref, other_ref, at)
        grad_mixed = stack_heads(gm_own_ref, gm_other_ref, at)
        q_rot, k_rot, value, probs = q_rot_ref[at4], k_rot_ref[at], value_ref[at], probs_ref[at4]
        grad_probs = dot_rows(grad_mixed, value)
        grad_value = dot_cols(probs.astype(bf16), grad_mixed).astype(bf16)
        inner = jnp.sum(grad_probs * probs, axis=-1, keepdims=True)
        grad_scores = (probs * (grad_probs - inner) * HD ** (-0.5)).astype(bf16)
        grad_q_rot = rotate_back(dot(grad_scores, k_rot), cos4, sin4)
        grad_k_rot = rotate_back(dot_cols(grad_scores, q_rot), cos, sin)
        grad_query = norm_back(query, grad_q_rot, q_gain_ref[...]).astype(bf16)
        grad_keys = norm_back(keys, grad_k_rot, k_gain_ref[...]).astype(bf16)
        for k in range(2):
            g_own_ref[at, k * HD : (k + 1) * HD] = grad_query[k * TRAJ : (k + 1) * TRAJ]
            g_other_ref[at, k * HD : (k + 1) * HD] = grad_query[(k + 2) * TRAJ : (k + 3) * TRAJ]
        g_own_ref[at, 2 * HD :] = jnp.where(first, grad_keys, grad_value)
        g_other_ref[at, 2 * HD :] = jnp.where(first, grad_value, grad_keys)
    for j in range(NY):
        span = outs[j].shape[0]
        left = tokens_of(normed_ref, slice(j * span, (j + 1) * span))
        other_out[j * span : (j + 1) * span] = dot_cols(left, g_other_ref[...]).astype(bf16)
        outs[j][...] = dot_cols(left, g_own_ref[...]).astype(bf16)


def by_trajectory(kernel, outs, ins):
    def spec(rows, cols):
        if rows == 0:
            return pl.BlockSpec(cols, lambda i: (0, 0))
        return pl.BlockSpec((rows, cols), lambda i: (i, 0))

    return pl.pallas_call(
        kernel,
        cost_estimate=pl.CostEstimate(
            flops=2 * 8 * NX * TRAJ * TRAJ * HD * 4, bytes_accessed=1 << 20, transcendentals=0
        ),
        grid=(NX,),
        out_shape=[jax.ShapeDtypeStruct((rows * NX, cols), kind) for rows, cols, kind in outs],
        in_specs=[pl.BlockSpec(memory_space=pltpu.SMEM)] + [spec(*entry) for entry in ins],
        out_specs=[spec(rows, cols) for rows, cols, _ in outs],
        compiler_params=pltpu.CompilerParams(vmem_limit_bytes=56 << 20),
    )


def grad_o_kernel(place_ref, part_ref, own_ref, other_ref, own_out, other_out):
    span = NZ * HD
    for j in range(NY):
        left = tokens_of(part_ref, slice(j * span, (j + 1) * span))
        at = pl.ds(pl.multiple_of(lax.rem(place_ref[0] + j, NY) * span, span), span)
        other_out[at] = dot_cols(left, other_ref[...]).astype(bf16)
        own_out[at] = dot_cols(left, own_ref[...]).astype(bf16)


def rope_tables():
    position = jnp.arange(TRAJ, dtype=jnp.int32).astype(f32)
    inverse = jnp.exp(
        jnp.arange(HD // 2, dtype=f32) * (-2.0 * jnp.log(jnp.float32(theta_base)) / HD)
    )
    angles = position[:, None] * inverse[None, :]
    cos, sin = jnp.cos(angles), jnp.sin(angles)
    return jnp.concatenate([cos, cos], axis=1), jnp.concatenate([-sin, sin], axis=1)


def after(values, *earlier):
    alone = not isinstance(values, (list, tuple))
    values = (values,) if alone else tuple(values)
    held = lax.optimization_barrier(values + earlier)[: len(values)]
    return held[0] if alone else list(held)


SAME_CORE = [[x * NC + c for x in range(NX)] for c in range(NC)]


def gather_x(value):
    return lax.all_gather(value, "dp", axis=0, tiled=True, axis_index_groups=SAME_CORE)


SAME_Z = [[y * NZ + z for y in range(NY)] for z in range(NZ)]


def scatter_y(value):
    return lax.psum_scatter(
        value, "fsdp", scatter_dimension=0, tiled=True, axis_index_groups=SAME_Z
    )


def scatter_x(value):
    return lax.psum_scatter(
        value, "dp", scatter_dimension=0, tiled=True, axis_index_groups=SAME_CORE
    )


def take_y(value, step):
    pairs = [(y * NZ + z, (y - step) % NY * NZ + z) for y in range(NY) for z in range(NZ)]
    return lax.ppermute(value, "fsdp", pairs)


def take_z(value, step):
    pairs = [(y * NZ + z, y * NZ + (z - step) % NZ) for y in range(NY) for z in range(NZ)]
    return lax.ppermute(value, "fsdp", pairs)


def other_core(value):
    return lax.ppermute(value, "dp", [(i, i ^ 1) for i in range(NX * NC)])


def owner_role(x):
    return x // (NX // 2)


def from_owner(value):
    n = NX * NC
    pairs = [(owner_role(d // NC) * n + d, (1 - owner_role(d // NC)) * n + d) for d in range(n)]
    return lax.ppermute(value, ("role", "dp"), pairs)


def to_owner(value):
    n = NX * NC
    pairs = [((1 - owner_role(d // NC)) * n + d, owner_role(d // NC) * n + d) for d in range(n)]
    return lax.ppermute(value, ("role", "dp"), pairs)


def spread_x(value, step):
    n = NX * NC
    pairs = [
        (owner_role(x) * n + x * NC + c, owner_role(x) * n + (x - step) % NX * NC + c)
        for x in range(NX)
        for c in range(NC)
    ]
    return lax.ppermute(value, ("role", "dp"), pairs)


def over_role(block, at_owner):
    return jnp.where(at_owner, block, from_owner(block))


def over_z(block):
    return jnp.concatenate([block] + [take_z(block, k) for k in range(1, NZ)], axis=0)


def over_y(plane):
    return [plane] + [take_y(plane, k) for k in range(1, NY)]


def add_core(own, theirs):
    span = own[0].shape[0]
    return [
        (own[k].astype(f32) + theirs[k * span : (k + 1) * span].astype(f32)).astype(bf16)
        for k in range(NY)
    ]


def add_y(terms):
    total = terms[0].astype(f32)
    for term in terms[1:]:
        total = total + term.astype(f32)
    span = total.shape[0] // NZ
    return [total[k * span : (k + 1) * span].astype(bf16) for k in range(NZ)]


def add_z(terms):
    total = terms[0].astype(f32)
    for k in range(1, NZ):
        total = total + take_z(terms[k], -k).astype(f32)
    return total.astype(bf16)


def add_role(term):
    return (term.astype(f32) + to_owner(term).astype(f32)).astype(bf16)


def share(total, x, role):
    copies = [total] + [spread_x(total, k) for k in range(1, NX)]
    items = []
    for sub in range(2):
        source = role * 2 + sub
        item = copies[0]
        for k in range(1, NX):
            item = jnp.where((source - x) % NX == k, copies[k], item)
        items.append(item)
    mine = jnp.concatenate(items, axis=0)
    return mine, other_core(mine)


def on_device(rows, cotangent, advantage, action, norm_gain, q_gain, k_gain, w_q, w_k, w_v, w_o):
    role = lax.axis_index("role")
    dp = lax.axis_index("dp")
    fsdp = lax.axis_index("fsdp")
    x, core = dp // NC, dp % NC
    y, z = fsdp // NZ, fsdp % NZ
    at_owner = role == owner_role(x)
    sub = x % 2
    width = 4 * HD
    half = 2 * HD
    first = core == 0
    place = jnp.stack([y, z]).astype(jnp.int32)
    flag = first.astype(jnp.int32)[None]

    q_part = lax.dynamic_slice(w_q, (0, sub * width + core * half), (HD, half))
    k_part = lax.dynamic_slice(w_k, (0, sub * HD), (HD, HD))
    v_part = lax.dynamic_slice(w_v, (0, sub * HD), (HD, HD))
    o_part = lax.dynamic_slice(w_o, (sub * width + core * half, 0), (half, HD)).T
    wide = half + HD
    kv_part = jnp.where(first, k_part, v_part)
    block_part = jnp.concatenate([q_part, kv_part, o_part], axis=1)
    block = over_role(block_part, at_owner)
    qkv_plane = over_z(block[:, :wide])

    rows_own, cot_own = rows[0], cotangent[0]
    gain = norm_gain[None]
    weight = (advantage[0] * action[0].astype(f32))[:, None]
    flat = (TRAJ, rows_own.shape[1])
    pair_own = call(rows_kernel, [((2 * TRAJ, flat[1]), bf16)], 5)(
        place, after(rows_own, block_part), gain, cot_own, weight
    )[0]
    pair = gather_x(pair_own)

    qkv_own = over_y(qkv_plane)
    qkv_first = other_core(qkv_plane)
    o_plane = over_z(after(block[:, wide:], qkv_first))
    o_first = other_core(o_plane)
    qkv_other = [qkv_first] + [other_core(after(piece, o_first)) for piece in qkv_own[1:]]
    o_late = after(o_plane, *qkv_own)
    o_near = [take_y(o_late, 1), take_y(o_late, 3)]

    tokens = pair.shape[0] // 2
    pair = pair.reshape(NX, 2, TRAJ, flat[1])
    cos_tab, sin_tab = rope_tables()
    proj_own, proj_other = call(
        project_kernel,
        [((tokens, wide), f32)] * 2,
        1 + 2 * NY,
        scalars=0,
        macs=tokens * flat[1] * 2 * wide,
        parts=[(0, flat[1])],
    )(after(pair, cos_tab, sin_tab), *qkv_own, *qkv_other)
    o_own = [o_plane, o_near[0], take_y(after(o_plane, proj_own), 2), o_near[1]]
    o_other = [o_first] + [other_core(after(piece, proj_own)) for piece in o_own[1:]]
    proj_own, proj_other = after([proj_own, proj_other], *o_near)
    shared = [(0, (1, HD)), (0, (1, HD)), (0, (TRAJ, HD)), (0, (TRAJ, HD))]
    tables = (q_gain[None], k_gain[None], cos_tab, sin_tab)
    kept = [(width, HD, bf16), (TRAJ, HD, bf16), (TRAJ, HD, bf16), (width, HD, f32)]
    q_rot, k_rot, value, probs, mixed_own, mixed_other = by_trajectory(
        attend_kernel,
        kept + [(TRAJ, half, bf16)] * 2,
        [(TRAJ, wide)] * 2 + shared,
    )(flag, proj_own, proj_other, *tables)

    span = NZ * HD
    go_own, go_cross = call(
        grad_o_kernel,
        [((NY * span, half), bf16)] * 2,
        4,
        macs=tokens * flat[1] * width,
        parts=[(1, flat[1])],
    )(place, after(pair, o_own[2], o_other[1], o_other[3]), mixed_own, mixed_other)
    go_theirs = after(other_core(go_cross), o_other[2])
    go_terms = scatter_y((go_own.astype(f32) + go_theirs.astype(f32)).astype(bf16))
    g_own, g_other, *gw_own, gw_cross = call(
        back_kernel,
        [((tokens, wide), bf16)] * 2
        + [((span, wide), bf16)] * NY
        + [((NY * span, wide), bf16)],
        13 + 2 * NY,
        macs=tokens * flat[1] * (width + 2 * wide),
        parts=[(0, flat[1]), (1, flat[1])],
        scratch_shapes=[pltpu.VMEM((tokens, half), bf16)] * 2,
    )(
        flag,
        *after([pair, pair], go_theirs),
        proj_own,
        proj_other,
        *tables,
        q_rot,
        k_rot,
        value,
        probs,
        *o_own,
        *o_other,
    )
    gw_theirs = other_core(gw_cross)
    terms = call(
        expand_kernel,
        [((2 * tokens, flat[1]), bf16)],
        4 + 4 * NY,
        scalars=0,
        macs=tokens * flat[1] * (width + 2 * wide),
    )(mixed_own, mixed_other, *after([g_own, g_other], gw_cross), *o_own, *o_other, *qkv_own, *qkv_other)[0]
    row_total = scatter_x(terms)

    gw_terms = after(add_core(gw_own, gw_theirs), terms)
    gw_near = [take_y(gw_terms[1], -1), take_y(gw_terms[3], -3)]
    go_terms = after(go_terms, *gw_near)
    go_term = add_z([go_terms[k * HD : (k + 1) * HD] for k in range(NZ)])
    gw_far = take_y(after(gw_terms[2], *gw_near), -2)
    gw_terms = add_y([gw_terms[0], *gw_near, after(gw_far, go_term)])
    gw_term = add_z(gw_terms)
    out_rows, grad_rows = call(
        finish_kernel, [(flat, bf16)] * 2, 6, scratch_shapes=[pltpu.VMEM(flat, f32)]
    )(place, rows_own, gain, cot_own, weight, row_total)
    total = add_role(jnp.concatenate([gw_term, go_term], axis=1))
    mine, theirs = share(total, x, role)
    g_0, g_1 = jnp.where(first, mine, theirs), jnp.where(first, theirs, mine)

    def pick(value, item, lo, hi):
        return value[item * HD : (item + 1) * HD, lo:hi].astype(f32)

    grad_w_q = jnp.concatenate(
        [pick(g, item, 0, half) for item in range(2) for g in (g_0, g_1)], axis=1
    )
    grad_w_k = jnp.concatenate([pick(g_0, item, half, wide) for item in range(2)], axis=1)
    grad_w_v = jnp.concatenate([pick(g_1, item, half, wide) for item in range(2)], axis=1)
    grad_w_o = jnp.concatenate(
        [pick(g, item, wide, wide + half).T for item in range(2) for g in (g_0, g_1)], axis=0
    )
    return (out_rows[None], grad_rows[None], grad_w_q, grad_w_k, grad_w_v, grad_w_o)


def solution(mesh):
    in_specs = (
        P(("dp", "fsdp"), "role", None),
        P(("dp", "fsdp"), "role", None),
        P(("dp", "fsdp"), "role"),
        P(("dp", "fsdp"), "role"),
        P(),
        P(),
        P(),
        P("fsdp", "role"),
        P("fsdp", "role"),
        P("fsdp", "role"),
        P("role", "fsdp"),
    )
    out_specs = (
        P(("dp", "fsdp"), "role", None),
        P(("dp", "fsdp"), "role", None),
        P("fsdp", "role"),
        P("fsdp", "role"),
        P("fsdp", "role"),
        P("role", "fsdp"),
    )
    return jax.shard_map(
        on_device, mesh=mesh, in_specs=in_specs, out_specs=out_specs, check_vma=False
    )
```
